512 devices in a mesh: dp: 32 (over y, z_hi), bal: 16 (over x, z_lo, core).
Axes of the slice: x: 4, y: 8, z: 8 (z_hi: 4, z_lo: 2; z = z_hi * 2 + z_lo), core: 2. Of those that a mesh axis runs over, the one named last changes fastest.
Arguments:
- counts: int32 [512], P(('dp', 'bal')), may hold values from 85 to 256, as said below
- rows: bfloat16 [131072, 1024], P(('dp', 'bal')), may hold values from -24 to 24
- cotangent: bfloat16 [131072, 512], P(('dp', 'bal')), may hold values from -6 to 6
- weight: bfloat16 [1024, 512], replicated, may hold values from -0.1875 to 0.1875
- gain: float32 [1024], replicated, may hold values from 0.1 to 1.9
- beta: float32 [1024], replicated, may hold values from -3 to 3
Outputs:
- grad_rows: bfloat16 [131072, 1024], P(('dp', 'bal'))
- grad_weight: float32 [1024, 512], P(('dp', 'bal'))
- grad_gain: float32 [1024], replicated
- grad_beta: float32 [1024], replicated
- grad_bias: float32 [512], replicated
The draws below stay inside these ranges and needn't reach their ends.
Inputs may be any that keep to these rules, and one draw needn't show every extreme that they name: `counts`: some sample has exactly 256 visible rows.
All inputs are finite; a program needn't handle non-finite values.
Results may differ from the reference program's by a relative error of at most 0.0029.
Values may be sent and summed in bfloat16 or wider, within the bound.
No kernel may reach another device: no remote copies, remote signals or barrier semaphores. Data moves between devices by JAX's collectives and lax.ppermute only.
A program may use at most 64 MiB of HBM per device.

```python
import jax
import jax.numpy as jnp
from jax import lax

D = 1024
E = 512
CAP = 256
NSAMP = 512
ROWS = 131072


def draw_counts(key, part):
    key = jax.random.fold_in(key, 17)
    primary, secondary = jax.random.split(key)
    values = jax.random.randint(primary, (NSAMP,), CAP // 3, CAP + 1, dtype=jnp.int32)
    chosen = jax.random.randint(secondary, (2,), 0, NSAMP, dtype=jnp.int32)
    values = values.at[chosen[1]].set(CAP // 3)
    values = values.at[chosen[0]].set(CAP)
    return values


def with_spikes(entries, own_key, source, target, shards_of, factor):
    def block_of(axis_at):
        return (jnp.arange(entries.shape[axis_at]) // (entries.shape[axis_at] // shards_of)).reshape((-1,) + (1,) * (entries.ndim - 1 - axis_at))

    one_side = jax.random.permutation(own_key, shards_of)[block_of(target)]
    other_side = (block_of(target) + shards_of // 2) % shards_of
    return jnp.where((block_of(source) == one_side) | (block_of(source) == other_side), factor * entries, entries)


def shard_levels(key, extent, shards, smallest, largest):
    level = 1.0
    for position, shards_of in shards:
        draws = jax.random.uniform(jax.random.fold_in(jax.random.fold_in(key, 6), position), (shards_of,), jnp.float32, smallest / len(shards), largest / len(shards))
        level = level * jnp.repeat(jnp.exp(draws), extent[position] // shards_of).reshape((-1,) + (1,) * (len(extent) - 1 - position))
    return level


def bell_draw(stream_key, extent, spread, most, cuts=(), kind=jnp.bfloat16):
    entries = spread * jax.random.normal(stream_key, extent, jnp.float32)
    if cuts:
        entries = entries * shard_levels(stream_key, extent, cuts, -0.22, 0.18)
    return jnp.clip(entries, -most, most).astype(kind)


def gaussian_with(stream_key, dims, scale, limit, cuts, heavy, kind=jnp.bfloat16):
    result = scale * jax.random.normal(stream_key, dims, jnp.float32)
    if cuts:
        result = result * shard_levels(stream_key, dims, cuts, -0.22, 0.18)
    return jnp.clip(with_spikes(result, jax.random.fold_in(stream_key, 3), *heavy), -limit, limit).astype(kind)


def setup_inputs(seed: int = 0) -> dict:
    keys = jax.random.split(jax.random.key(seed), 7)
    counts = draw_counts(jax.random.fold_in(keys[6], 71), 0)
    rows = gaussian_with(keys[1], (ROWS, D), 1.0, 24.0, ((0, 512),), (0, 1, 512, 6.0))
    cotangent = bell_draw(keys[2], (ROWS, E), 1.0, 6.0, ((0, 512),))
    weight = bell_draw(keys[3], (D, E), D ** -0.5, 0.1875)
    gain = jnp.clip(1.0 + 0.18 * jax.random.normal(keys[4], (D,), jnp.float32), 0.1, 1.9)
    beta = bell_draw(keys[5], (D,), 0.5, 3.0, (), jnp.float32)
    return {"counts": counts, "rows": rows, "cotangent": cotangent, "weight": weight, "gain": gain, "beta": beta}


epsilon = 1e-06

def row_grads(x_rows, cot_rows, live, gain, beta, weight):
    row_mask = (jnp.arange(x_rows.shape[0]) < live)[:, None]
    x_float = x_rows.astype(jnp.float32)
    centred = x_float - lax.optimization_barrier(jnp.mean(x_float, axis=1, keepdims=True))
    inv_std = lax.rsqrt(lax.optimization_barrier(jnp.mean(centred * centred, axis=1, keepdims=True)) + epsilon)
    normed = centred * inv_std
    hidden = (normed * gain + beta).astype(jnp.bfloat16)
    hidden = jnp.where(row_mask, hidden, jnp.zeros_like(hidden))
    cot_live = jnp.where(row_mask, cot_rows, jnp.zeros_like(cot_rows))
    grad_w = lax.dot_general(hidden, cot_live, (((0,), (0,)), ((), ())), preferred_element_type=jnp.float32)
    grad_h = lax.dot_general(cot_live, weight, (((1,), (1,)), ((), ())), preferred_element_type=jnp.float32)
    grad_gain = lax.optimization_barrier(jnp.sum(grad_h * normed, axis=0))
    grad_beta = lax.optimization_barrier(jnp.sum(grad_h, axis=0))
    grad_bias = lax.optimization_barrier(jnp.sum(cot_live.astype(jnp.float32), axis=0))
    scaled = grad_h * gain
    grad_x = inv_std * (scaled - lax.optimization_barrier(jnp.mean(scaled, axis=1, keepdims=True)) - normed * lax.optimization_barrier(jnp.mean(scaled * normed, axis=1, keepdims=True)))
    grad_x = jnp.where(row_mask, grad_x, jnp.zeros_like(grad_x)).astype(jnp.bfloat16)
    return (grad_x, grad_w, grad_gain, grad_beta, grad_bias)

def reference(counts, rows, cotangent, weight, gain, beta):
    sample_rows = rows.reshape(NSAMP, CAP, D)
    sample_cot = cotangent.reshape(NSAMP, CAP, E)

    def advance(sums, item):
        x_rows, cot_rows, live = item
        grad_x, grad_w, grad_gain, grad_beta, grad_bias = row_grads(x_rows, cot_rows, live, gain, beta, weight)
        return ((sums[0] + grad_w, sums[1] + grad_gain, sums[2] + grad_beta, sums[3] + grad_bias), grad_x)
    start_sums = (jnp.zeros((D, E), jnp.float32), jnp.zeros((D,), jnp.float32), jnp.zeros((D,), jnp.float32), jnp.zeros((E,), jnp.float32))
    sums, grads = lax.scan(advance, start_sums, (sample_rows, sample_cot, counts))
    scale = lax.rsqrt(jnp.sum(counts.astype(jnp.float32)))
    return (grads.reshape(ROWS, D), sums[0] * scale, sums[1] * scale, sums[2] * scale, sums[3] * scale)
```

```python
import jax
import jax.numpy as jnp
from jax import lax
from jax.sharding import PartitionSpec as P

epsilon = 1e-06


def row_grads(x_rows, cot_rows, live, gain, beta, weight):
    row_mask = (jnp.arange(x_rows.shape[0]) < live)[:, None]
    x_float = x_rows.astype(jnp.float32)
    centred = x_float - jnp.mean(x_float, axis=1, keepdims=True)
    inv_std = lax.rsqrt(jnp.mean(centred * centred, axis=1, keepdims=True) + epsilon)
    normed = centred * inv_std
    hidden = (normed * gain + beta).astype(jnp.bfloat16)
    hidden = jnp.where(row_mask, hidden, jnp.zeros_like(hidden))
    cot_live = jnp.where(row_mask, cot_rows, jnp.zeros_like(cot_rows))
    grad_w = lax.dot_general(
        hidden, cot_live, (((0,), (0,)), ((), ())), preferred_element_type=jnp.float32
    )
    grad_h = lax.dot_general(
        cot_live, weight, (((1,), (1,)), ((), ())), preferred_element_type=jnp.float32
    )
    grad_gain = jnp.sum(grad_h * normed, axis=0)
    grad_beta = jnp.sum(grad_h, axis=0)
    grad_bias = jnp.sum(cot_live.astype(jnp.float32), axis=0)
    scaled = grad_h * gain
    grad_x = inv_std * (
        scaled
        - jnp.mean(scaled, axis=1, keepdims=True)
        - normed * jnp.mean(scaled * normed, axis=1, keepdims=True)
    )
    grad_x = jnp.where(row_mask, grad_x, jnp.zeros_like(grad_x)).astype(jnp.bfloat16)
    return (grad_x, grad_w, grad_gain, grad_beta, grad_bias)


def count_row(count, width):
    high = count // 256
    low = count - high * 256
    lane = jnp.arange(width)
    return jnp.where(lane == 0, high, jnp.where(lane == 1, low, 0)).astype(jnp.float32)[None, :]


def make_body(dp, bal):
    def body(counts, rows, cotangent, weight, gain, beta):
        width = rows.shape[1]
        decoder = cotangent.shape[1]
        own = width // (dp * bal)
        per_vector = width // decoder
        my_count = counts[0]
        grad_rows, grad_w, grad_gain, grad_beta, grad_bias = row_grads(
            rows, cotangent, my_count, gain, beta, weight
        )

        def pad_rows(small):
            return jnp.pad(small, ((0, -small.shape[0] % 8), (0, 0)))

        small = pad_rows(
            jnp.concatenate(
                [
                    grad_gain.reshape(per_vector, decoder),
                    grad_beta.reshape(per_vector, decoder),
                    grad_bias[None, :],
                    count_row(my_count, decoder),
                ]
            )
        )
        blocks = grad_w.reshape(dp, bal, own, decoder).transpose(1, 0, 2, 3)
        blocks = blocks.reshape(bal, dp * own, decoder)
        first = jnp.concatenate(
            [blocks, jnp.broadcast_to(small[None], (bal,) + small.shape)], axis=1
        ).astype(jnp.bfloat16)
        first = lax.all_to_all(first, "bal", 0, 0, tiled=True)
        first = jnp.sum(first.astype(jnp.float32), axis=0)
        part = first[: dp * own].reshape(dp, own, decoder)
        small = first[dp * own :]
        at = 2 * per_vector + 1
        count = small[at, 0].astype(jnp.int32) * 256 + small[at, 1].astype(jnp.int32)
        small = jnp.concatenate([small[:at], count_row(count, decoder)])
        second = jnp.concatenate(
            [part, jnp.broadcast_to(small[None], (dp,) + small.shape)], axis=1
        ).astype(jnp.bfloat16)
        second = lax.all_to_all(second, "dp", 0, 0, tiled=True)
        second = jnp.sum(second.astype(jnp.float32), axis=0)
        at = own + 2 * per_vector
        total = second[at + 1, 0] * 256.0 + second[at + 1, 1]
        second = second[: at + 1] * lax.rsqrt(total)
        return (
            grad_rows,
            second[:own],
            second[own : own + per_vector].reshape(width),
            second[own + per_vector : at].reshape(width),
            second[at],
        )

    return body


def solution(mesh):
    placed = (P(("dp", "bal")), P(("dp", "bal"), None), P(("dp", "bal"), None), P(), P(), P())
    return jax.shard_map(
        make_body(mesh.shape["dp"], mesh.shape["bal"]),
        mesh=mesh,
        in_specs=placed,
        out_specs=(P(("dp", "bal"), None), P(("dp", "bal"), None), P(), P(), P()),
        check_vma=False,
    )
```

```python
import functools

import jax
import jax.numpy as jnp
from jax import lax
from jax.experimental import pallas as pl
from jax.experimental.pallas import tpu as pltpu
from jax.sharding import PartitionSpec as P

epsilon = 1e-06
LANES = 128
SUBLANES = 8
COUNT_BASE = 256


def normalise(x_rows):
    x_float = x_rows.astype(jnp.float32)
    centred = x_float - jnp.mean(x_float, axis=1, keepdims=True)
    inv_std = lax.rsqrt(jnp.mean(centred * centred, axis=1, keepdims=True) + epsilon)
    return centred * inv_std, inv_std


def live_cotangent(count_ref, cot_ref):
    row = lax.broadcasted_iota(jnp.int32, cot_ref.shape, 0)
    cot = cot_ref[...]
    return jnp.where(row < count_ref[0], cot, jnp.zeros_like(cot))


def backproject(cot_live, weight_ref):
    return lax.dot_general(
        cot_live,
        weight_ref[...],
        (((1,), (1,)), ((), ())),
        preferred_element_type=jnp.float32,
    )


def count_row(count, width):
    high = jnp.floor(count * (1.0 / COUNT_BASE))
    low = count - high * COUNT_BASE
    lane = lax.broadcasted_iota(jnp.int32, (1, width), 1)
    return jnp.where(lane == 0, high, jnp.where(lane == 1, low, 0.0))


def count_of(row):
    lane = lax.broadcasted_iota(jnp.int32, row.shape, 1)
    place = jnp.where(lane == 0, float(COUNT_BASE), jnp.where(lane == 1, 1.0, 0.0))
    return jnp.sum(row * place, axis=1, keepdims=True)


def sums_kernel(
    dp,
    bal,
    count_ref,
    x_hbm,
    cot_hbm,
    weight_hbm,
    gain_hbm,
    beta_hbm,
    out_ref,
    x_ref,
    cot_ref,
    weight_ref,
    gain_ref,
    beta_ref,
    grad_w,
    small,
    arrived,
):
    copies = [
        pltpu.make_async_copy(source, target, arrived.at[index])
        for index, (source, target) in enumerate(
            (
                (x_hbm, x_ref),
                (gain_hbm, gain_ref),
                (beta_hbm, beta_ref),
                (cot_hbm, cot_ref),
                (weight_hbm, weight_ref),
            )
        )
    ]
    for copy in copies:
        copy.start()
    width, decoder = weight_ref.shape
    own = width // (dp * bal)
    vectors = width // decoder
    copies[0].wait()
    normed, _ = normalise(x_ref[...])
    for copy in copies[1:4]:
        copy.wait()
    hidden = (normed * gain_ref[...] + beta_ref[...]).astype(jnp.bfloat16)
    cot_live = live_cotangent(count_ref, cot_ref)
    product = lax.dot_general(
        hidden, cot_live, (((0,), (0,)), ((), ())), preferred_element_type=jnp.float32
    )
    for tile in range(decoder // LANES):
        grad_w[tile] = product[:, tile * LANES : (tile + 1) * LANES]
    copies[4].wait()
    grad_h = backproject(cot_live, weight_ref)
    grad_gain = jnp.sum(grad_h * normed, axis=0, keepdims=True)
    grad_beta = jnp.sum(grad_h, axis=0, keepdims=True)
    small[...] = jnp.zeros_like(small)
    for part in range(vectors):
        at = slice(part * decoder, (part + 1) * decoder)
        small[part : part + 1] = grad_gain[:, at]
        small[vectors + part : vectors + part + 1] = grad_beta[:, at]
    at = 2 * vectors
    small[at : at + 1] = jnp.sum(cot_live.astype(jnp.float32), axis=0, keepdims=True)
    small[at + 1 : at + 2] = count_row(
        jnp.full((1, 1), count_ref[0], jnp.int32).astype(jnp.float32), decoder
    )
    small_sent = small[...].astype(jnp.bfloat16)
    for owner in range(bal):
        for row in range(own):
            rows = pl.ds(owner * own + row, dp, stride=bal * own)
            for tile in range(decoder // LANES):
                out_ref[owner, row * dp : (row + 1) * dp, tile * LANES : (tile + 1) * LANES] = (
                    grad_w[tile, rows, :].astype(jnp.bfloat16)
                )
        out_ref[owner, own * dp :, :] = small_sent


def regroup_kernel(dp, own, got_ref, out_ref, spread):
    decoder = got_ref.shape[2]
    rows = out_ref.shape[1]
    total = jnp.sum(got_ref[...].astype(jnp.float32), axis=0)
    kept = rows - own
    small = total[own * dp :]
    count = count_row(count_of(small[kept - 1 : kept]), decoder)
    for tile in range(decoder // LANES):
        at = slice(tile * LANES, (tile + 1) * LANES)
        for row in range(own):
            spread[tile, pl.ds(row, dp, stride=rows), :] = total[row * dp : (row + 1) * dp, at]
        for row in range(kept):
            line = count[:, at] if row == kept - 1 else small[row : row + 1, at]
            spread[tile, pl.ds(own + row, dp, stride=rows), :] = jnp.broadcast_to(
                line, (dp, LANES)
            )
        out_ref[:, :, at] = spread[tile].reshape(dp, rows, LANES).astype(jnp.bfloat16)


def finish_kernel(own, vectors, got_ref, weight_ref, gain_ref, beta_ref, bias_ref):
    total = jnp.sum(got_ref[...].astype(jnp.float32), axis=0)
    decoder = total.shape[1]
    at = own + 2 * vectors
    scaled = total * lax.rsqrt(count_of(total[at + 1 : at + 2]))
    weight_ref[...] = scaled[:own]
    for part in range(vectors):
        lanes = slice(part * decoder, (part + 1) * decoder)
        gain_ref[:, lanes] = scaled[own + part : own + part + 1]
        beta_ref[:, lanes] = scaled[own + vectors + part : own + vectors + part + 1]
    bias_ref[...] = scaled[at : at + 1]


def rows_kernel(count_ref, x_ref, cot_ref, weight_ref, gain_ref, out_ref):
    normed, inv_std = normalise(x_ref[...])
    scaled = backproject(live_cotangent(count_ref, cot_ref), weight_ref) * gain_ref[...]
    out_ref[...] = (
        inv_std
        * (
            scaled
            - jnp.mean(scaled, axis=1, keepdims=True)
            - normed * jnp.mean(scaled * normed, axis=1, keepdims=True)
        )
    ).astype(jnp.bfloat16)


VMEM = pl.BlockSpec(memory_space=pltpu.VMEM)
HBM = pl.BlockSpec(memory_space=pltpu.HBM)
SMEM = pl.BlockSpec(memory_space=pltpu.SMEM)
PARAMS = pltpu.CompilerParams(vmem_limit_bytes=32 * 1024 * 1024)


def cost(flops, transfers):
    return pl.CostEstimate(flops=flops, bytes_accessed=transfers, transcendentals=0)


def make_body(dp, bal):
    def body(counts, rows, cotangent, weight, gain, beta):
        count, width = rows.shape
        decoder = cotangent.shape[1]
        own = width // (dp * bal)
        vectors = width // decoder
        tiles = decoder // LANES
        kept = 2 * vectors + 2
        sent = own * dp + SUBLANES
        gain = gain.reshape(1, width)
        beta = beta.reshape(1, width)
        whole = (rows, cotangent, weight, gain, beta)
        work = 2 * count * width * decoder
        first = pl.pallas_call(
            functools.partial(sums_kernel, dp, bal),
            out_shape=jax.ShapeDtypeStruct((bal, sent, decoder), jnp.bfloat16),
            in_specs=[SMEM] + [HBM] * 5,
            out_specs=VMEM,
            scratch_shapes=[
                pltpu.VMEM(rows.shape, rows.dtype),
                pltpu.VMEM(cotangent.shape, cotangent.dtype),
                pltpu.VMEM(weight.shape, weight.dtype),
                pltpu.VMEM((1, width), jnp.float32),
                pltpu.VMEM((1, width), jnp.float32),
                pltpu.VMEM((tiles, width, LANES), jnp.float32),
                pltpu.VMEM((SUBLANES, decoder), jnp.float32),
                pltpu.SemaphoreType.DMA((5,)),
            ],
            compiler_params=PARAMS,
            cost_estimate=cost(2 * work, 3000000),
            name="sums",
        )(counts, *(pltpu.with_memory_space_constraint(each, pltpu.HBM) for each in whole))
        first = lax.all_to_all(first, "bal", 0, 0, tiled=True)
        second = pl.pallas_call(
            functools.partial(regroup_kernel, dp, own),
            out_shape=jax.ShapeDtypeStruct((dp, own + kept, decoder), jnp.bfloat16),
            in_specs=[VMEM],
            out_specs=VMEM,
            scratch_shapes=[pltpu.VMEM((tiles, dp * (own + kept), LANES), jnp.float32)],
            compiler_params=PARAMS,
            cost_estimate=cost(1000000, 1500000),
            name="regroup",
        )(first)
        second, rows, cotangent = lax.optimization_barrier((second, rows, cotangent))
        grad_rows = pl.pallas_call(
            rows_kernel,
            out_shape=jax.ShapeDtypeStruct((count, width), jnp.bfloat16),
            in_specs=[SMEM] + [VMEM] * 4,
            out_specs=VMEM,
            compiler_params=PARAMS,
            cost_estimate=cost(work, 3000000),
            name="rows",
        )(counts, rows, cotangent, weight, gain)
        second = lax.all_to_all(second, "dp", 0, 0, tiled=True)
        vector = jax.ShapeDtypeStruct((1, width), jnp.float32)
        grad_weight, grad_gain, grad_beta, grad_bias = pl.pallas_call(
            functools.partial(finish_kernel, own, vectors),
            out_shape=(
                jax.ShapeDtypeStruct((own, decoder), jnp.float32),
                vector,
                vector,
                jax.ShapeDtypeStruct((1, decoder), jnp.float32),
            ),
            in_specs=[VMEM],
            out_specs=(VMEM,) * 4,
            compiler_params=PARAMS,
            cost_estimate=cost(1000000, 300000),
            name="finish",
        )(second)
        return (
            grad_rows,
            grad_weight,
            grad_gain.reshape(width),
            grad_beta.reshape(width),
            grad_bias.reshape(decoder),
        )

    return body


def solution(mesh):
    placed = (P(("dp", "bal")), P(("dp", "bal"), None), P(("dp", "bal"), None), P(), P(), P())
    return jax.shard_map(
        make_body(mesh.shape["dp"], mesh.shape["bal"]),
        mesh=mesh,
        in_specs=placed,
        out_specs=(P(("dp", "bal"), None), P(("dp", "bal"), None), P(), P(), P()),
        check_vma=False,
    )
```

```python
import functools

import jax
import jax.numpy as jnp
from jax import lax
from jax.experimental import pallas as pl
from jax.experimental.pallas import tpu as pltpu
from jax.sharding import PartitionSpec as P

epsilon = 1e-06
LANES = 128
SUBLANES = 8
CORES = 2
COUNT_BASE = 256


def ring(step, size):
    return min(step % size, -step % size)


def bal_order(bal):
    return sorted(
        range(bal), key=lambda at: (-2 * ring(at // 4, bal // 4) - at // 2 % 2 - 0.5 * (at % 2), at)
    )


def dp_order(dp):
    size_y, size_z = dp // 4, 4
    start = (size_y // 2, size_z // 2)

    def distance(at):
        return ring(at // size_z - start[0], size_y) + 2 * ring(at % size_z - start[1], size_z)

    return sorted(range(dp), key=lambda at: (distance(at), at))


def normalise(x_rows):
    x_float = x_rows.astype(jnp.float32)
    centred = x_float - jnp.mean(x_float, axis=1, keepdims=True)
    inv_std = lax.rsqrt(jnp.mean(centred * centred, axis=1, keepdims=True) + epsilon)
    return centred * inv_std, inv_std


def live_cotangent(count_ref, cot_ref):
    row = lax.broadcasted_iota(jnp.int32, cot_ref.shape, 0)
    cot = cot_ref[...]
    return jnp.where(row < count_ref[0], cot, jnp.zeros_like(cot))


def backproject(cot_live, weight_ref):
    return lax.dot_general(
        cot_live,
        weight_ref[...],
        (((1,), (1,)), ((), ())),
        preferred_element_type=jnp.float32,
    )


def project(hidden, cot_live):
    return lax.dot_general(
        hidden, cot_live, (((0,), (0,)), ((), ())), preferred_element_type=jnp.float32
    )


def start_copies(arrived, *pairs):
    copies = [
        pltpu.make_async_copy(source, target, arrived.at[index])
        for index, (source, target) in enumerate(pairs)
    ]
    for copy in copies:
        copy.start()
    return copies


def count_row(count, width):
    high = jnp.floor(count * (1.0 / COUNT_BASE))
    low = count - high * COUNT_BASE
    lane = lax.broadcasted_iota(jnp.int32, (1, width), 1)
    return jnp.where(lane == 0, high, jnp.where(lane == 1, low, 0.0))


def count_of(row):
    lane = lax.broadcasted_iota(jnp.int32, row.shape, 1)
    place = jnp.where(lane == 0, float(COUNT_BASE), jnp.where(lane == 1, 1.0, 0.0))
    return jnp.sum(row * place, axis=1, keepdims=True)


def prepare_kernel(
    count_ref,
    x_hbm,
    cot_hbm,
    gain_hbm,
    beta_hbm,
    send_ref,
    hidden_ref,
    normed_ref,
    live_ref,
    x_ref,
    cot_ref,
    gain_ref,
    beta_ref,
    arrived,
):
    copies = start_copies(
        arrived,
        (x_hbm, x_ref),
        (gain_hbm, gain_ref),
        (beta_hbm, beta_ref),
        (cot_hbm, cot_ref),
    )
    half = hidden_ref.shape[2]
    copies[0].wait()
    normed, _ = normalise(x_ref[...])
    normed_ref[...] = normed
    for copy in copies[1:]:
        copy.wait()
    hidden = (normed * gain_ref[...] + beta_ref[...]).astype(jnp.bfloat16)
    for part in range(CORES):
        hidden_ref[part] = hidden[:, part * half : (part + 1) * half]
    cot_live = live_cotangent(count_ref, cot_ref)
    live_ref[...] = cot_live
    send_ref[:, half:] = cot_live
    send_ref[:, :half] = hidden_ref[1 - lax.axis_index("bal") % CORES]


def own_kernel(
    count_ref, hidden_ref, normed_ref, live_ref, weight_hbm, product_ref, small, weight_ref, arrived
):
    copies = start_copies(arrived, (weight_hbm, weight_ref))
    width, decoder = weight_ref.shape
    vectors = width // decoder
    cot_live = live_ref[...]
    product_ref[...] = project(hidden_ref[lax.axis_index("bal") % CORES], cot_live)
    copies[0].wait()
    grad_h = backproject(cot_live, weight_ref)
    grad_gain = jnp.sum(grad_h * normed_ref[...], axis=0, keepdims=True)
    grad_beta = jnp.sum(grad_h, axis=0, keepdims=True)
    small[...] = jnp.zeros_like(small)
    for part in range(vectors):
        at = slice(part * decoder, (part + 1) * decoder)
        small[part : part + 1] = grad_gain[:, at]
        small[vectors + part : vectors + part + 1] = grad_beta[:, at]
    at = 2 * vectors
    small[at : at + 1] = jnp.sum(cot_live.astype(jnp.float32), axis=0, keepdims=True)
    small[at + 1 : at + 2] = count_row(
        jnp.full((1, 1), count_ref[0], jnp.int32).astype(jnp.float32), decoder
    )


def pair_kernel(dp, bal, own, got_ref, product_ref, small_ref, out_ref, grad_w):
    span = bal * own
    pitch = span + 1
    peers = dp // CORES
    half, decoder = product_ref.shape
    product = product_ref[...] + project(got_ref[:, :half], got_ref[:, half:])
    for tile in range(decoder // LANES):
        at = slice(tile * LANES, (tile + 1) * LANES)
        for peer in range(peers):
            grad_w[tile, peer * pitch : peer * pitch + span] = product[
                peer * span : (peer + 1) * span, at
            ]
    small = small_ref[...].astype(jnp.bfloat16)
    for place, owner in enumerate(bal_order(bal)):
        for tile in range(decoder // LANES):
            at = slice(tile * LANES, (tile + 1) * LANES)
            for row in range(own):
                rows = pl.ds(owner * own + row, peers, stride=pitch)
                out_ref[place, row * peers : (row + 1) * peers, at] = grad_w[
                    tile, rows, :
                ].astype(jnp.bfloat16)
        out_ref[place, own * peers :, :] = small


def regroup_kernel(dp, own, got_ref, out_ref, spread):
    bal, _, decoder = got_ref.shape
    rows = out_ref.shape[1]
    kept = rows - own
    peers = dp // CORES
    halves = [0.0] * CORES
    for place, member in enumerate(bal_order(bal)):
        halves[member % CORES] += got_ref[place].astype(jnp.float32)
    small = sum(part[own * peers :] for part in halves)
    count = count_row(count_of(small[kept - 1 : kept]), decoder)
    for tile in range(decoder // LANES):
        at = slice(tile * LANES, (tile + 1) * LANES)
        for core in range(CORES):
            for row in range(own):
                spread[tile, pl.ds(core * peers * rows + row, peers, stride=rows), :] = halves[
                    core
                ][row * peers : (row + 1) * peers, at]
        for row in range(kept):
            line = count[:, at] if row == kept - 1 else small[row : row + 1, at]
            spread[tile, pl.ds(own + row, dp, stride=rows), :] = jnp.broadcast_to(
                line, (dp, LANES)
            )
        for place, peer in enumerate(dp_order(dp)):
            out_ref[place, :, at] = spread[tile, peer * rows : (peer + 1) * rows].astype(
                jnp.bfloat16
            )


def finish_kernel(own, vectors, got_ref, weight_ref, gain_ref, beta_ref, bias_ref):
    total = jnp.sum(got_ref[...].astype(jnp.float32), axis=0)
    decoder = total.shape[1]
    at = own + 2 * vectors
    scaled = total * lax.rsqrt(count_of(total[at + 1 : at + 2]))
    weight_ref[...] = scaled[:own]
    for part in range(vectors):
        lanes = slice(part * decoder, (part + 1) * decoder)
        gain_ref[:, lanes] = scaled[own + part : own + part + 1]
        beta_ref[:, lanes] = scaled[own + vectors + part : own + vectors + part + 1]
    bias_ref[...] = scaled[at : at + 1]


def rows_kernel(
    count_ref,
    x_hbm,
    cot_hbm,
    weight_hbm,
    gain_hbm,
    out_ref,
    x_ref,
    cot_ref,
    weight_ref,
    gain_ref,
    arrived,
):
    copies = start_copies(
        arrived,
        (x_hbm, x_ref),
        (gain_hbm, gain_ref),
        (cot_hbm, cot_ref),
        (weight_hbm, weight_ref),
    )
    copies[0].wait()
    normed, inv_std = normalise(x_ref[...])
    for copy in copies[1:]:
        copy.wait()
    scaled = backproject(live_cotangent(count_ref, cot_ref), weight_ref) * gain_ref[...]
    out_ref[...] = (
        inv_std
        * (
            scaled
            - jnp.mean(scaled, axis=1, keepdims=True)
            - normed * jnp.mean(scaled * normed, axis=1, keepdims=True)
        )
    ).astype(jnp.bfloat16)


VMEM = pl.BlockSpec(memory_space=pltpu.VMEM)
SMEM = pl.BlockSpec(memory_space=pltpu.SMEM)
HBM = pl.BlockSpec(memory_space=pltpu.HBM)
PARAMS = pltpu.CompilerParams(vmem_limit_bytes=32 * 1024 * 1024)


def cost(flops, transfers):
    return pl.CostEstimate(flops=flops, bytes_accessed=transfers, transcendentals=0)


def in_hbm(*arrays):
    return tuple(pltpu.with_memory_space_constraint(each, pltpu.HBM) for each in arrays)


def scratch_of(*arrays):
    return [pltpu.VMEM(each.shape, each.dtype) for each in arrays] + [
        pltpu.SemaphoreType.DMA((len(arrays),))
    ]


def exchange(blocks, axis, order):
    return lax.all_to_all(blocks, axis, 0, 0, tiled=True, axis_index_groups=[order])


def make_body(dp, bal):
    def body(counts, rows, cotangent, weight, gain, beta):
        count, width = rows.shape
        decoder = cotangent.shape[1]
        half = width // CORES
        own = width // (dp * bal)
        vectors = width // decoder
        tiles = decoder // LANES
        kept = 2 * vectors + 2
        peers = dp // CORES
        gain = gain.reshape(1, width)
        beta = beta.reshape(1, width)
        work = 2 * count * width * decoder
        shape = jax.ShapeDtypeStruct
        send, hidden, normed, live = pl.pallas_call(
            prepare_kernel,
            out_shape=(
                shape((count, half + decoder), jnp.bfloat16),
                shape((CORES, count, half), jnp.bfloat16),
                shape((count, width), jnp.float32),
                shape((count, decoder), jnp.bfloat16),
            ),
            in_specs=[SMEM] + [HBM] * 4,
            out_specs=(VMEM,) * 4,
            scratch_shapes=scratch_of(rows, cotangent, gain, beta),
            compiler_params=PARAMS,
            cost_estimate=cost(20 * count * width, 3000000),
            name="prepare",
        )(counts, *in_hbm(rows, cotangent, gain, beta))
        got = lax.ppermute(send, "bal", [(member, member ^ 1) for member in range(bal)])
        product, small = pl.pallas_call(
            own_kernel,
            out_shape=(
                shape((half, decoder), jnp.float32),
                shape((SUBLANES, decoder), jnp.float32),
            ),
            in_specs=[SMEM] + [VMEM] * 3 + [HBM],
            out_specs=(VMEM,) * 2,
            scratch_shapes=scratch_of(weight),
            compiler_params=PARAMS,
            cost_estimate=cost(3 * work // 2, 3000000),
            name="own",
        )(counts, hidden, normed, live, *in_hbm(weight))
        first = pl.pallas_call(
            functools.partial(pair_kernel, dp, bal, own),
            out_shape=shape((bal, own * peers + SUBLANES, decoder), jnp.bfloat16),
            in_specs=[VMEM] * 3,
            out_specs=VMEM,
            scratch_shapes=[pltpu.VMEM((tiles, peers * (bal * own + 1), LANES), jnp.float32)],
            compiler_params=PARAMS,
            cost_estimate=cost(work // 2, 2000000),
            name="pair",
        )(got, product, small)
        first = exchange(first, "bal", bal_order(bal))
        second = pl.pallas_call(
            functools.partial(regroup_kernel, dp, own),
            out_shape=shape((dp, own + kept, decoder), jnp.bfloat16),
            in_specs=[VMEM],
            out_specs=VMEM,
            scratch_shapes=[pltpu.VMEM((tiles, dp * (own + kept), LANES), jnp.float32)],
            compiler_params=PARAMS,
            cost_estimate=cost(1000000, 1500000),
            name="regroup",
        )(first)
        second, rows, cotangent = lax.optimization_barrier((second, rows, cotangent))
        grad_rows = pl.pallas_call(
            rows_kernel,
            out_shape=shape((count, width), jnp.bfloat16),
            in_specs=[SMEM] + [HBM] * 4,
            out_specs=VMEM,
            scratch_shapes=scratch_of(rows, cotangent, weight, gain),
            compiler_params=PARAMS,
            cost_estimate=cost(work, 3000000),
            name="rows",
        )(counts, *in_hbm(rows, cotangent, weight, gain))
        second = exchange(second, "dp", dp_order(dp))
        vector = shape((1, width), jnp.float32)
        grad_weight, grad_gain, grad_beta, grad_bias = pl.pallas_call(
            functools.partial(finish_kernel, own, vectors),
            out_shape=(
                shape((own, decoder), jnp.float32),
                vector,
                vector,
                shape((1, decoder), jnp.float32),
            ),
            in_specs=[VMEM],
            out_specs=(VMEM,) * 4,
            compiler_params=PARAMS,
            cost_estimate=cost(1000000, 300000),
            name="finish",
        )(second)
        return (
            grad_rows,
            grad_weight,
            grad_gain.reshape(width),
            grad_beta.reshape(width),
            grad_bias.reshape(decoder),
        )

    return body


def solution(mesh):
    placed = (P(("dp", "bal")), P(("dp", "bal"), None), P(("dp", "bal"), None), P(), P(), P())
    return jax.shard_map(
        make_body(mesh.shape["dp"], mesh.shape["bal"]),
        mesh=mesh,
        in_specs=placed,
        out_specs=(P(("dp", "bal"), None), P(("dp", "bal"), None), P(), P(), P()),
        check_vma=False,
    )
```

```python
import functools

import jax
import jax.numpy as jnp
from jax import lax
from jax.experimental import pallas as pl
from jax.experimental.pallas import tpu as pltpu
from jax.sharding import PartitionSpec as P

epsilon = 1e-06
LANES = 128
SUBLANES = 8
CORES = 2
COUNT_BASE = 256


def ring(step, size):
    return min(step % size, -step % size)


def bal_order(bal):
    return sorted(
        range(bal), key=lambda at: (-2 * ring(at // 4, bal // 4) - at // 2 % 2 - 0.5 * (at % 2), at)
    )


def dp_order(dp):
    size_y, size_z = dp // 4, 4
    start = (size_y // 2, size_z // 2)

    def distance(at):
        return ring(at // size_z - start[0], size_y) + 2 * ring(at % size_z - start[1], size_z)

    return sorted(range(dp), key=lambda at: (distance(at), at))


def normalise(x_rows):
    x_float = x_rows.astype(jnp.float32)
    centred = x_float - jnp.mean(x_float, axis=1, keepdims=True)
    inv_std = lax.rsqrt(jnp.mean(centred * centred, axis=1, keepdims=True) + epsilon)
    return centred * inv_std, inv_std


def live_cotangent(count_ref, cot_ref):
    row = lax.broadcasted_iota(jnp.int32, cot_ref.shape, 0)
    cot = cot_ref[...]
    return jnp.where(row < count_ref[0], cot, jnp.zeros_like(cot))


def backproject(cot_live, weight_ref):
    return lax.dot_general(
        cot_live,
        weight_ref[...],
        (((1,), (1,)), ((), ())),
        preferred_element_type=jnp.float32,
    )


def project(hidden, cot_live):
    return lax.dot_general(
        hidden, cot_live, (((0,), (0,)), ((), ())), preferred_element_type=jnp.float32
    )


def start_copies(arrived, *pairs):
    copies = [
        pltpu.make_async_copy(source, target, arrived.at[index])
        for index, (source, target) in enumerate(pairs)
    ]
    for copy in copies:
        copy.start()
    return copies


def count_row(count):
    high = jnp.floor(count * (1.0 / COUNT_BASE))
    low = count - high * COUNT_BASE
    lane = lax.broadcasted_iota(jnp.int32, (1, LANES), 1)
    return jnp.where(lane == 0, high, jnp.where(lane == 1, low, 0.0))


def count_of(row):
    lane = lax.broadcasted_iota(jnp.int32, row.shape, 1)
    place = jnp.where(lane == 0, float(COUNT_BASE), jnp.where(lane == 1, 1.0, 0.0))
    return jnp.sum(row * place, axis=1, keepdims=True)


def put_lines(ref, start, vector):
    for line in range(vector.shape[1] // LANES):
        ref[start + line : start + line + 1] = vector[:, line * LANES : (line + 1) * LANES]


def prepare_kernel(
    count_ref,
    x_hbm,
    cot_hbm,
    gain_hbm,
    beta_hbm,
    send_ref,
    hidden_ref,
    normed_ref,
    live_ref,
    x_ref,
    cot_ref,
    gain_ref,
    beta_ref,
    arrived,
):
    copies = start_copies(
        arrived,
        (x_hbm, x_ref),
        (gain_hbm, gain_ref),
        (beta_hbm, beta_ref),
        (cot_hbm, cot_ref),
    )
    half = hidden_ref.shape[2]
    copies[0].wait()
    normed, _ = normalise(x_ref[...])
    normed_ref[...] = normed
    for copy in copies[1:]:
        copy.wait()
    hidden = (normed * gain_ref[...] + beta_ref[...]).astype(jnp.bfloat16)
    for part in range(CORES):
        hidden_ref[part] = hidden[:, part * half : (part + 1) * half]
    cot_live = live_cotangent(count_ref, cot_ref)
    live_ref[...] = cot_live
    send_ref[:, half:] = cot_live
    send_ref[:, :half] = hidden_ref[1 - lax.axis_index("bal") % CORES]


def own_kernel(
    count_ref, hidden_ref, normed_ref, live_ref, weight_hbm, product_ref, small, weight_ref, arrived
):
    copies = start_copies(arrived, (weight_hbm, weight_ref))
    width, decoder = weight_ref.shape
    cot_live = live_ref[...]
    product_ref[...] = project(hidden_ref[lax.axis_index("bal") % CORES], cot_live)
    copies[0].wait()
    grad_h = backproject(cot_live, weight_ref)
    grad_gain = jnp.sum(grad_h * normed_ref[...], axis=0, keepdims=True)
    grad_bias = jnp.sum(cot_live.astype(jnp.float32), axis=0, keepdims=True)
    small[...] = jnp.zeros_like(small)
    put_lines(small, 0, grad_gain)
    put_lines(small, width // LANES, grad_bias)
    at = (width + decoder) // LANES
    small[at : at + 1] = count_row(
        jnp.full((1, 1), count_ref[0], jnp.int32).astype(jnp.float32)
    )


def pair_kernel(dp, bal, own, got_ref, product_ref, small_ref, out_ref, grad_w):
    span = bal * own
    pitch = span + 1
    peers = dp // CORES
    half, decoder = product_ref.shape
    product = product_ref[...] + project(got_ref[:, :half], got_ref[:, half:])
    for tile in range(decoder // LANES):
        at = slice(tile * LANES, (tile + 1) * LANES)
        for peer in range(peers):
            grad_w[tile, peer * pitch : peer * pitch + span] = product[
                peer * span : (peer + 1) * span, at
            ]
    small = small_ref[...].astype(jnp.bfloat16)
    tiles = decoder // LANES
    for place, owner in enumerate(bal_order(bal)):
        for tile in range(tiles):
            for row in range(own):
                rows = pl.ds(owner * own + row, peers, stride=pitch)
                at = (tile * own + row) * peers
                out_ref[place, at : at + peers, :] = grad_w[tile, rows, :].astype(jnp.bfloat16)
        out_ref[place, tiles * own * peers :, :] = small


def regroup_kernel(dp, lines, at_count, got_ref, out_ref, spread):
    bal = got_ref.shape[0]
    peers = dp // CORES
    halves = [0.0] * CORES
    for place, member in enumerate(bal_order(bal)):
        halves[member % CORES] += got_ref[place].astype(jnp.float32)
    small = sum(part[lines * peers :] for part in halves)
    line = lax.broadcasted_iota(jnp.int32, small.shape, 0)
    count = count_of(small[at_count : at_count + 1])
    small = jnp.where(line == at_count, count_row(count), small).astype(jnp.bfloat16)
    for core in range(CORES):
        for row in range(lines):
            spread[pl.ds(core * peers * lines + row, peers, stride=lines), :] = halves[core][
                row * peers : (row + 1) * peers
            ]
    for place, peer in enumerate(dp_order(dp)):
        out_ref[place, :lines, :] = spread[peer * lines : (peer + 1) * lines].astype(jnp.bfloat16)
        out_ref[place, lines:, :] = small


def finish_kernel(got_ref, projection_ref, weight_ref, gain_ref, beta_ref, bias_ref):
    width, decoder = projection_ref.shape
    own, tiles = weight_ref.shape[0], decoder // LANES
    total = jnp.sum(got_ref[...].astype(jnp.float32), axis=0)
    at_gain = own * tiles
    at_bias = at_gain + width // LANES
    at_count = at_bias + tiles
    scaled = total * lax.rsqrt(count_of(total[at_count : at_count + 1]))

    def joined(start, lines):
        return jnp.concatenate(
            [scaled[start + line : start + line + 1] for line in range(lines)], axis=1
        )

    for tile in range(tiles):
        weight_ref[:, tile * LANES : (tile + 1) * LANES] = scaled[tile * own : (tile + 1) * own]
    gain_ref[...] = joined(at_gain, width // LANES)
    bias = joined(at_bias, tiles)
    bias_ref[...] = bias
    row = lax.broadcasted_iota(jnp.int32, (SUBLANES, decoder), 0)
    terms = jnp.zeros((SUBLANES, decoder), jnp.float32)
    for term in range(3):
        part = bias.astype(jnp.bfloat16).astype(jnp.float32)
        terms = jnp.where(row == term, part, terms)
        bias = bias - part
    beta_ref[...] = jnp.sum(
        backproject(terms.astype(jnp.bfloat16), projection_ref), axis=0, keepdims=True
    )


def rows_kernel(
    count_ref,
    x_hbm,
    cot_hbm,
    weight_hbm,
    gain_hbm,
    out_ref,
    x_ref,
    cot_ref,
    weight_ref,
    gain_ref,
    arrived,
):
    copies = start_copies(
        arrived,
        (x_hbm, x_ref),
        (gain_hbm, gain_ref),
        (cot_hbm, cot_ref),
        (weight_hbm, weight_ref),
    )
    copies[0].wait()
    normed, inv_std = normalise(x_ref[...])
    for copy in copies[1:]:
        copy.wait()
    scaled = backproject(live_cotangent(count_ref, cot_ref), weight_ref) * gain_ref[...]
    out_ref[...] = (
        inv_std
        * (
            scaled
            - jnp.mean(scaled, axis=1, keepdims=True)
            - normed * jnp.mean(scaled * normed, axis=1, keepdims=True)
        )
    ).astype(jnp.bfloat16)


VMEM = pl.BlockSpec(memory_space=pltpu.VMEM)
SMEM = pl.BlockSpec(memory_space=pltpu.SMEM)
HBM = pl.BlockSpec(memory_space=pltpu.HBM)
PARAMS = pltpu.CompilerParams(vmem_limit_bytes=32 * 1024 * 1024)


def cost(flops, transfers):
    return pl.CostEstimate(flops=flops, bytes_accessed=transfers, transcendentals=0)


def in_hbm(*arrays):
    return tuple(pltpu.with_memory_space_constraint(each, pltpu.HBM) for each in arrays)


def scratch_of(*arrays):
    return [pltpu.VMEM(each.shape, each.dtype) for each in arrays] + [
        pltpu.SemaphoreType.DMA((len(arrays),))
    ]


def exchange(blocks, axis, order):
    return lax.all_to_all(blocks, axis, 0, 0, tiled=True, axis_index_groups=[order])


def make_body(dp, bal):
    def body(counts, rows, cotangent, weight, gain, beta):
        count, width = rows.shape
        decoder = cotangent.shape[1]
        half = width // CORES
        own = width // (dp * bal)
        tiles = decoder // LANES
        lines = tiles * own
        at_count = (width + decoder) // LANES
        kept = -(-(at_count + 1) // SUBLANES) * SUBLANES
        peers = dp // CORES
        gain = gain.reshape(1, width)
        beta = beta.reshape(1, width)
        work = 2 * count * width * decoder
        shape = jax.ShapeDtypeStruct
        send, hidden, normed, live = pl.pallas_call(
            prepare_kernel,
            out_shape=(
                shape((count, half + decoder), jnp.bfloat16),
                shape((CORES, count, half), jnp.bfloat16),
                shape((count, width), jnp.float32),
                shape((count, decoder), jnp.bfloat16),
            ),
            in_specs=[SMEM] + [HBM] * 4,
            out_specs=(VMEM,) * 4,
            scratch_shapes=scratch_of(rows, cotangent, gain, beta),
            compiler_params=PARAMS,
            cost_estimate=cost(20 * count * width, 3000000),
            name="prepare",
        )(counts, *in_hbm(rows, cotangent, gain, beta))
        got = lax.ppermute(send, "bal", [(member, member ^ 1) for member in range(bal)])
        product, small = pl.pallas_call(
            own_kernel,
            out_shape=(
                shape((half, decoder), jnp.float32),
                shape((kept, LANES), jnp.float32),
            ),
            in_specs=[SMEM] + [VMEM] * 3 + [HBM],
            out_specs=(VMEM,) * 2,
            scratch_shapes=scratch_of(weight),
            compiler_params=PARAMS,
            cost_estimate=cost(3 * work // 2, 3000000),
            name="own",
        )(counts, hidden, normed, live, *in_hbm(weight))
        first = pl.pallas_call(
            functools.partial(pair_kernel, dp, bal, own),
            out_shape=shape((bal, lines * peers + kept, LANES), jnp.bfloat16),
            in_specs=[VMEM] * 3,
            out_specs=VMEM,
            scratch_shapes=[pltpu.VMEM((tiles, peers * (bal * own + 1), LANES), jnp.float32)],
            compiler_params=PARAMS,
            cost_estimate=cost(work // 2, 2000000),
            name="pair",
        )(got, product, small)
        first = exchange(first, "bal", bal_order(bal))
        second = pl.pallas_call(
            functools.partial(regroup_kernel, dp, lines, at_count),
            out_shape=shape((dp, lines + kept, LANES), jnp.bfloat16),
            in_specs=[VMEM],
            out_specs=VMEM,
            scratch_shapes=[pltpu.VMEM((dp * lines, LANES), jnp.float32)],
            compiler_params=PARAMS,
            cost_estimate=cost(1000000, 1500000),
            name="regroup",
        )(first)
        second, rows, cotangent = lax.optimization_barrier((second, rows, cotangent))
        grad_rows = pl.pallas_call(
            rows_kernel,
            out_shape=shape((count, width), jnp.bfloat16),
            in_specs=[SMEM] + [HBM] * 4,
            out_specs=VMEM,
            scratch_shapes=scratch_of(rows, cotangent, weight, gain),
            compiler_params=PARAMS,
            cost_estimate=cost(work, 3000000),
            name="rows",
        )(counts, *in_hbm(rows, cotangent, weight, gain))
        second = exchange(second, "dp", dp_order(dp))
        vector = shape((1, width), jnp.float32)
        grad_weight, grad_gain, grad_beta, grad_bias = pl.pallas_call(
            finish_kernel,
            out_shape=(
                shape((own, decoder), jnp.float32),
                vector,
                vector,
                shape((1, decoder), jnp.float32),
            ),
            in_specs=[VMEM] * 2,
            out_specs=(VMEM,) * 4,
            compiler_params=PARAMS,
            cost_estimate=cost(1000000, 300000),
            name="finish",
        )(second, weight)
        return (
            grad_rows,
            grad_weight,
            grad_gain.reshape(width),
            grad_beta.reshape(width),
            grad_bias.reshape(decoder),
        )

    return body


def solution(mesh):
    placed = (P(("dp", "bal")), P(("dp", "bal"), None), P(("dp", "bal"), None), P(), P(), P())
    return jax.shard_map(
        make_body(mesh.shape["dp"], mesh.shape["bal"]),
        mesh=mesh,
        in_specs=placed,
        out_specs=(P(("dp", "bal"), None), P(("dp", "bal"), None), P(), P(), P()),
        check_vma=False,
    )
```

```python
import functools

import jax
import jax.numpy as jnp
from jax import lax
from jax.experimental import pallas as pl
from jax.experimental.pallas import tpu as pltpu
from jax.sharding import PartitionSpec as P

epsilon = 1e-06
LANES = 128
SUBLANES = 8
CORES = 2
PART_ROWS = 64
COUNT_BASE = 256


def ring(step, size):
    return min(step % size, -step % size)


def bal_order(bal):
    return sorted(
        range(bal), key=lambda at: (-2 * ring(at // 4, bal // 4) - at // 2 % 2 - 0.5 * (at % 2), at)
    )


def dp_order(dp):
    size_y, size_z = dp // 4, 4
    start = (size_y // 2, size_z // 2)

    def distance(at):
        return ring(at // size_z - start[0], size_y) + 2 * ring(at % size_z - start[1], size_z)

    return sorted(range(dp), key=lambda at: (distance(at), at))


def normalise(x_rows):
    x_float = x_rows.astype(jnp.float32)
    centred = x_float - jnp.mean(x_float, axis=1, keepdims=True)
    inv_std = lax.rsqrt(jnp.mean(centred * centred, axis=1, keepdims=True) + epsilon)
    return centred * inv_std, inv_std


def live_cotangent(count_ref, cot_ref):
    row = lax.broadcasted_iota(jnp.int32, cot_ref.shape, 0)
    cot = cot_ref[...]
    return jnp.where(row < count_ref[0], cot, jnp.zeros_like(cot))


def backproject(cot_live, weight_ref):
    return lax.dot_general(
        cot_live,
        weight_ref[...],
        (((1,), (1,)), ((), ())),
        preferred_element_type=jnp.float32,
    )


def project(hidden, cot_live):
    return lax.dot_general(
        hidden, cot_live, (((0,), (0,)), ((), ())), preferred_element_type=jnp.float32
    )


def start_copies(arrived, *pairs):
    copies = [
        pltpu.make_async_copy(source, target, arrived.at[index])
        for index, (source, target) in enumerate(pairs)
    ]
    for copy in copies:
        copy.start()
    return copies


def count_row(count):
    high = jnp.floor(count * (1.0 / COUNT_BASE))
    low = count - high * COUNT_BASE
    lane = lax.broadcasted_iota(jnp.int32, (1, LANES), 1)
    return jnp.where(lane == 0, high, jnp.where(lane == 1, low, 0.0))


def count_of(row):
    lane = lax.broadcasted_iota(jnp.int32, row.shape, 1)
    place = jnp.where(lane == 0, float(COUNT_BASE), jnp.where(lane == 1, 1.0, 0.0))
    return jnp.sum(row * place, axis=1, keepdims=True)


def put_lines(ref, start, vector):
    for line in range(vector.shape[1] // LANES):
        ref[start + line : start + line + 1] = vector[:, line * LANES : (line + 1) * LANES]


def prepare_kernel(
    count_ref,
    x_hbm,
    cot_hbm,
    weight_hbm,
    gain_hbm,
    beta_hbm,
    send_ref,
    hidden_ref,
    normed_ref,
    inv_std_ref,
    weight_ref,
    x_ref,
    cot_ref,
    gain_ref,
    beta_ref,
    arrived,
):
    half = hidden_ref.shape[1]
    copies = start_copies(
        arrived,
        (x_hbm, x_ref),
        (gain_hbm, gain_ref),
        (beta_hbm, beta_ref),
        (cot_hbm, cot_ref),
        (weight_hbm, weight_ref),
    )
    first_core = lax.axis_index("bal") % CORES == 0
    copies[0].wait()
    normed, inv_std = normalise(x_ref[...])
    normed_ref[...] = normed
    inv_std_ref[...] = inv_std
    for copy in copies[1:3]:
        copy.wait()
    hidden = (normed * gain_ref[...] + beta_ref[...]).astype(jnp.bfloat16)
    low, high = hidden[:, :half], hidden[:, half:]
    hidden_ref[...] = jnp.where(first_core, low, high)
    send_ref[:, :half] = jnp.where(first_core, high, low)
    copies[3].wait()
    send_ref[:, half:] = live_cotangent(count_ref, cot_ref)
    copies[4].wait()


def own_kernel(
    count_ref,
    hidden_ref,
    normed_ref,
    inv_std_ref,
    send_ref,
    weight_ref,
    gain_ref,
    product_ref,
    small,
    rows_hbm,
    rows_ref,
    left,
):
    width, decoder = weight_ref.shape
    cot_live = send_ref[:, hidden_ref.shape[1] :]
    grad_h = backproject(cot_live, weight_ref)
    count = rows_ref.shape[0]
    copies = []
    for start in range(0, count, PART_ROWS):
        part = slice(start, start + PART_ROWS)
        normed = normed_ref[part]
        scaled = grad_h[part] * gain_ref[...]
        rows_ref[part] = (
            inv_std_ref[part]
            * (
                scaled
                - jnp.mean(scaled, axis=1, keepdims=True)
                - normed * jnp.mean(scaled * normed, axis=1, keepdims=True)
            )
        ).astype(jnp.bfloat16)
        copies.append(
            pltpu.make_async_copy(
                rows_ref.at[part], rows_hbm.at[part], left.at[start // PART_ROWS]
            )
        )
        copies[-1].start()
    grad_gain = jnp.sum(grad_h * normed_ref[...], axis=0, keepdims=True)
    grad_bias = jnp.sum(cot_live.astype(jnp.float32), axis=0, keepdims=True)
    small[...] = jnp.zeros_like(small)
    put_lines(small, 0, grad_gain)
    put_lines(small, width // LANES, grad_bias)
    at = (width + decoder) // LANES
    small[at : at + 1] = count_row(
        jnp.full((1, 1), count_ref[0], jnp.int32).astype(jnp.float32)
    )
    product_ref[...] = project(hidden_ref[...], cot_live)
    for copy in copies:
        copy.wait()


def pair_kernel(dp, bal, own, got_ref, product_ref, small_ref, out_ref, grad_w):
    span = bal * own
    pitch = span + 1
    peers = dp // CORES
    half, decoder = product_ref.shape
    product = product_ref[...] + project(got_ref[:, :half], got_ref[:, half:])
    for tile in range(decoder // LANES):
        at = slice(tile * LANES, (tile + 1) * LANES)
        for peer in range(peers):
            grad_w[tile, peer * pitch : peer * pitch + span] = product[
                peer * span : (peer + 1) * span, at
            ]
    small = small_ref[...].astype(jnp.bfloat16)
    tiles = decoder // LANES
    for place, owner in enumerate(bal_order(bal)):
        for tile in range(tiles):
            for row in range(own):
                rows = pl.ds(owner * own + row, peers, stride=pitch)
                at = (tile * own + row) * peers
                out_ref[place, at : at + peers, :] = grad_w[tile, rows, :].astype(jnp.bfloat16)
        out_ref[place, tiles * own * peers :, :] = small


def regroup_kernel(dp, lines, at_count, got_ref, out_ref, spread):
    bal = got_ref.shape[0]
    peers = dp // CORES
    halves = [0.0] * CORES
    for place, member in enumerate(bal_order(bal)):
        halves[member % CORES] += got_ref[place].astype(jnp.float32)
    small = sum(part[lines * peers :] for part in halves)
    line = lax.broadcasted_iota(jnp.int32, small.shape, 0)
    count = count_of(small[at_count : at_count + 1])
    small = jnp.where(line == at_count, count_row(count), small).astype(jnp.bfloat16)
    for core in range(CORES):
        for row in range(lines):
            spread[pl.ds(core * peers * lines + row, peers, stride=lines), :] = halves[core][
                row * peers : (row + 1) * peers
            ]
    for place, peer in enumerate(dp_order(dp)):
        out_ref[place, :lines, :] = spread[peer * lines : (peer + 1) * lines].astype(jnp.bfloat16)
        out_ref[place, lines:, :] = small


def finish_kernel(got_ref, projection_ref, weight_ref, gain_ref, beta_ref, bias_ref):
    width, decoder = projection_ref.shape
    own, tiles = weight_ref.shape[0], decoder // LANES
    total = jnp.sum(got_ref[...].astype(jnp.float32), axis=0)
    at_gain = own * tiles
    at_bias = at_gain + width // LANES
    at_count = at_bias + tiles
    scaled = total * lax.rsqrt(count_of(total[at_count : at_count + 1]))

    def joined(start, lines):
        return jnp.concatenate(
            [scaled[start + line : start + line + 1] for line in range(lines)], axis=1
        )

    for tile in range(tiles):
        weight_ref[:, tile * LANES : (tile + 1) * LANES] = scaled[tile * own : (tile + 1) * own]
    gain_ref[...] = joined(at_gain, width // LANES)
    bias = joined(at_bias, tiles)
    bias_ref[...] = bias
    row = lax.broadcasted_iota(jnp.int32, (SUBLANES, decoder), 0)
    terms = jnp.zeros((SUBLANES, decoder), jnp.float32)
    for term in range(3):
        part = bias.astype(jnp.bfloat16).astype(jnp.float32)
        terms = jnp.where(row == term, part, terms)
        bias = bias - part
    beta_ref[...] = jnp.sum(
        backproject(terms.astype(jnp.bfloat16), projection_ref), axis=0, keepdims=True
    )


VMEM = pl.BlockSpec(memory_space=pltpu.VMEM)
SMEM = pl.BlockSpec(memory_space=pltpu.SMEM)
HBM = pl.BlockSpec(memory_space=pltpu.HBM)
PARAMS = pltpu.CompilerParams(vmem_limit_bytes=32 * 1024 * 1024)


def cost(flops, transfers):
    return pl.CostEstimate(flops=flops, bytes_accessed=transfers, transcendentals=0)


def in_hbm(*arrays):
    return tuple(pltpu.with_memory_space_constraint(each, pltpu.HBM) for each in arrays)


def exchange(blocks, axis, order):
    return lax.all_to_all(blocks, axis, 0, 0, tiled=True, axis_index_groups=[order])


def make_body(dp, bal):
    def body(counts, rows, cotangent, weight, gain, beta):
        count, width = rows.shape
        decoder = cotangent.shape[1]
        half = width // CORES
        own = width // (dp * bal)
        tiles = decoder // LANES
        lines = tiles * own
        at_count = (width + decoder) // LANES
        kept = -(-(at_count + 1) // SUBLANES) * SUBLANES
        peers = dp // CORES
        gain = gain.reshape(1, width)
        beta = beta.reshape(1, width)
        work = 2 * count * width * decoder
        shape = jax.ShapeDtypeStruct
        send, hidden, normed, inv_std, weight_near = pl.pallas_call(
            prepare_kernel,
            out_shape=(
                shape((count, half + decoder), jnp.bfloat16),
                shape((count, half), jnp.bfloat16),
                shape((count, width), jnp.float32),
                shape((count, 1), jnp.float32),
                shape(weight.shape, weight.dtype),
            ),
            in_specs=[SMEM] + [HBM] * 5,
            out_specs=(VMEM,) * 5,
            scratch_shapes=[
                pltpu.VMEM(rows.shape, rows.dtype),
                pltpu.VMEM(cotangent.shape, cotangent.dtype),
                pltpu.VMEM(gain.shape, gain.dtype),
                pltpu.VMEM(beta.shape, beta.dtype),
                pltpu.SemaphoreType.DMA((5,)),
            ],
            compiler_params=PARAMS,
            cost_estimate=cost(20 * count * width, 3000000),
            name="prepare",
        )(counts, *in_hbm(rows, cotangent, weight, gain, beta))
        got = lax.ppermute(send, "bal", [(member, member ^ 1) for member in range(bal)])
        product, small, grad_rows = pl.pallas_call(
            own_kernel,
            out_shape=(
                shape((half, decoder), jnp.float32),
                shape((kept, LANES), jnp.float32),
                shape(rows.shape, rows.dtype),
            ),
            in_specs=[SMEM] + [VMEM] * 6,
            out_specs=(VMEM, VMEM, HBM),
            scratch_shapes=[
                pltpu.VMEM(rows.shape, rows.dtype),
                pltpu.SemaphoreType.DMA((count // PART_ROWS,)),
            ],
            compiler_params=PARAMS,
            cost_estimate=cost(3 * work // 2, 3000000),
            name="own",
        )(counts, hidden, normed, inv_std, send, weight_near, gain)
        first = pl.pallas_call(
            functools.partial(pair_kernel, dp, bal, own),
            out_shape=shape((bal, lines * peers + kept, LANES), jnp.bfloat16),
            in_specs=[VMEM] * 3,
            out_specs=VMEM,
            scratch_shapes=[pltpu.VMEM((tiles, peers * (bal * own + 1), LANES), jnp.float32)],
            compiler_params=PARAMS,
            cost_estimate=cost(work // 2, 2000000),
            name="pair",
        )(got, product, small)
        first = exchange(first, "bal", bal_order(bal))
        second = pl.pallas_call(
            functools.partial(regroup_kernel, dp, lines, at_count),
            out_shape=shape((dp, lines + kept, LANES), jnp.bfloat16),
            in_specs=[VMEM],
            out_specs=VMEM,
            scratch_shapes=[pltpu.VMEM((dp * lines, LANES), jnp.float32)],
            compiler_params=PARAMS,
            cost_estimate=cost(1000000, 1500000),
            name="regroup",
        )(first)
        second = exchange(second, "dp", dp_order(dp))
        vector = shape((1, width), jnp.float32)
        grad_weight, grad_gain, grad_beta, grad_bias = pl.pallas_call(
            finish_kernel,
            out_shape=(
                shape((own, decoder), jnp.float32),
                vector,
                vector,
                shape((1, decoder), jnp.float32),
            ),
            in_specs=[VMEM] * 2,
            out_specs=(VMEM,) * 4,
            compiler_params=PARAMS,
            cost_estimate=cost(1000000, 300000),
            name="finish",
        )(second, weight_near)
        return (
            grad_rows,
            grad_weight,
            grad_gain.reshape(width),
            grad_beta.reshape(width),
            grad_bias.reshape(decoder),
        )

    return body


def solution(mesh):
    placed = (P(("dp", "bal")), P(("dp", "bal"), None), P(("dp", "bal"), None), P(), P(), P())
    return jax.shard_map(
        make_body(mesh.shape["dp"], mesh.shape["bal"]),
        mesh=mesh,
        in_specs=placed,
        out_specs=(P(("dp", "bal"), None), P(("dp", "bal"), None), P(), P(), P()),
        check_vma=False,
    )
```

```python
import functools

import jax
import jax.numpy as jnp
from jax import lax
from jax.experimental import pallas as pl
from jax.experimental.pallas import tpu as pltpu
from jax.sharding import PartitionSpec as P

epsilon = 1e-06
LANES = 128
SUBLANES = 8
CORES = 2
PART_ROWS = 64
COUNT_BASE = 256


def ring(step, size):
    return min(step % size, -step % size)


def bal_order(bal):
    return sorted(
        range(bal), key=lambda at: (-2 * ring(at // 4, bal // 4) - at // 2 % 2 - 0.5 * (at % 2), at)
    )


def dp_order(dp):
    size_y, size_z = dp // 4, 4
    start = (size_y // 2, size_z // 2)

    def distance(at):
        return ring(at // size_z - start[0], size_y) + 2 * ring(at % size_z - start[1], size_z)

    return sorted(range(dp), key=lambda at: (distance(at), at))


def normalise(x_rows):
    x_float = x_rows.astype(jnp.float32)
    centred = x_float - jnp.mean(x_float, axis=1, keepdims=True)
    inv_std = lax.rsqrt(jnp.mean(centred * centred, axis=1, keepdims=True) + epsilon)
    return centred * inv_std, inv_std


def live_cotangent(count_ref, cot_ref):
    row = lax.broadcasted_iota(jnp.int32, cot_ref.shape, 0)
    cot = cot_ref[...]
    return jnp.where(row < count_ref[0], cot, jnp.zeros_like(cot))


def backproject(cot_live, weight_ref):
    return lax.dot_general(
        cot_live,
        weight_ref[...],
        (((1,), (1,)), ((), ())),
        preferred_element_type=jnp.float32,
    )


def project(hidden, cot_live):
    return lax.dot_general(
        hidden, cot_live, (((0,), (0,)), ((), ())), preferred_element_type=jnp.float32
    )


def start_copies(arrived, *pairs):
    copies = [
        pltpu.make_async_copy(source, target, arrived.at[index])
        for index, (source, target) in enumerate(pairs)
    ]
    for copy in copies:
        copy.start()
    return copies


def count_row(count):
    high = jnp.floor(count * (1.0 / COUNT_BASE))
    low = count - high * COUNT_BASE
    lane = lax.broadcasted_iota(jnp.int32, (1, LANES), 1)
    return jnp.where(lane == 0, high, jnp.where(lane == 1, low, 0.0))


def count_of(row):
    lane = lax.broadcasted_iota(jnp.int32, row.shape, 1)
    place = jnp.where(lane == 0, float(COUNT_BASE), jnp.where(lane == 1, 1.0, 0.0))
    return jnp.sum(row * place, axis=1, keepdims=True)


def put_lines(ref, start, vector):
    for line in range(vector.shape[1] // LANES):
        ref[start + line : start + line + 1] = vector[:, line * LANES : (line + 1) * LANES]


def prepare_kernel(
    count_ref,
    x_hbm,
    cot_hbm,
    weight_hbm,
    gain_hbm,
    beta_hbm,
    send_ref,
    hidden_ref,
    normed_ref,
    inv_std_ref,
    weight_ref,
    x_ref,
    cot_ref,
    gain_ref,
    beta_ref,
    arrived,
):
    half = hidden_ref.shape[1]
    copies = start_copies(
        arrived,
        (x_hbm, x_ref),
        (gain_hbm, gain_ref),
        (beta_hbm, beta_ref),
        (cot_hbm, cot_ref),
        (weight_hbm, weight_ref),
    )
    first_core = lax.axis_index("bal") % CORES == 0
    copies[0].wait()
    normed, inv_std = normalise(x_ref[...])
    normed_ref[...] = normed
    inv_std_ref[...] = inv_std
    for copy in copies[1:3]:
        copy.wait()
    hidden = (normed * gain_ref[...] + beta_ref[...]).astype(jnp.bfloat16)
    low, high = hidden[:, :half], hidden[:, half:]
    hidden_ref[...] = jnp.where(first_core, low, high)
    send_ref[:, :half] = jnp.where(first_core, high, low)
    copies[3].wait()
    send_ref[:, half:] = live_cotangent(count_ref, cot_ref)
    copies[4].wait()


def own_kernel(
    count_ref,
    hidden_ref,
    normed_ref,
    inv_std_ref,
    send_ref,
    weight_ref,
    gain_ref,
    product_ref,
    small,
    rows_hbm,
    rows_ref,
    left,
):
    width, decoder = weight_ref.shape
    cot_live = send_ref[:, hidden_ref.shape[1] :]
    grad_h = backproject(cot_live, weight_ref)
    count = rows_ref.shape[0]
    copies = []
    for start in range(0, count, PART_ROWS):
        part = slice(start, start + PART_ROWS)
        normed = normed_ref[part]
        scaled = grad_h[part] * gain_ref[...]
        rows_ref[part] = (
            inv_std_ref[part]
            * (
                scaled
                - jnp.mean(scaled, axis=1, keepdims=True)
                - normed * jnp.mean(scaled * normed, axis=1, keepdims=True)
            )
        ).astype(jnp.bfloat16)
        copies.append(
            pltpu.make_async_copy(
                rows_ref.at[part], rows_hbm.at[part], left.at[start // PART_ROWS]
            )
        )
        copies[-1].start()
    grad_gain = jnp.sum(grad_h * normed_ref[...], axis=0, keepdims=True)
    grad_bias = jnp.sum(cot_live.astype(jnp.float32), axis=0, keepdims=True)
    small[...] = jnp.zeros_like(small)
    put_lines(small, 0, grad_gain)
    put_lines(small, width // LANES, grad_bias)
    at = (width + decoder) // LANES
    small[at : at + 1] = count_row(
        jnp.full((1, 1), count_ref[0], jnp.int32).astype(jnp.float32)
    )
    product_ref[...] = project(hidden_ref[...], cot_live)
    for copy in copies:
        copy.wait()


def pair_kernel(dp, bal, own, got_ref, product_ref, small_ref, out_ref, grad_w):
    span = bal * own
    pitch = span + 1
    peers = dp // CORES
    half, decoder = product_ref.shape
    product = product_ref[...] + project(got_ref[:, :half], got_ref[:, half:])
    for tile in range(decoder // LANES):
        at = slice(tile * LANES, (tile + 1) * LANES)
        for peer in range(peers):
            grad_w[tile, peer * pitch : peer * pitch + span] = product[
                peer * span : (peer + 1) * span, at
            ]
    small = small_ref[...].astype(jnp.bfloat16)
    tiles = decoder // LANES
    for place, owner in enumerate(bal_order(bal)):
        for tile in range(tiles):
            for row in range(own):
                rows = pl.ds(owner * own + row, peers, stride=pitch)
                at = (tile * own + row) * peers
                out_ref[place, at : at + peers, :] = grad_w[tile, rows, :].astype(jnp.bfloat16)
        out_ref[place, tiles * own * peers :, :] = small


def regroup_kernel(dp, lines, at_count, got_ref, out_ref, spread):
    bal = got_ref.shape[0]
    peers = dp // CORES
    halves = [0.0] * CORES
    for place, member in enumerate(bal_order(bal)):
        halves[member % CORES] += got_ref[place].astype(jnp.float32)
    small = sum(part[lines * peers :] for part in halves)
    line = lax.broadcasted_iota(jnp.int32, small.shape, 0)
    count = count_of(small[at_count : at_count + 1])
    small = jnp.where(line == at_count, count_row(count), small).astype(jnp.bfloat16)
    for core in range(CORES):
        for row in range(lines):
            spread[pl.ds(core * peers * lines + row, peers, stride=lines), :] = halves[core][
                row * peers : (row + 1) * peers
            ]
    for place, peer in enumerate(dp_order(dp)):
        out_ref[place, :lines, :] = spread[peer * lines : (peer + 1) * lines].astype(jnp.bfloat16)
        out_ref[place, lines:, :] = small


def finish_kernel(got_ref, projection_ref, weight_ref, gain_ref, beta_ref, bias_ref):
    width, decoder = projection_ref.shape
    own, tiles = weight_ref.shape[0], decoder // LANES
    total = jnp.sum(got_ref[...].astype(jnp.float32), axis=0)
    at_gain = own * tiles
    at_bias = at_gain + width // LANES
    at_count = at_bias + tiles
    scaled = total * lax.rsqrt(count_of(total[at_count : at_count + 1]))

    def joined(start, lines):
        return jnp.concatenate(
            [scaled[start + line : start + line + 1] for line in range(lines)], axis=1
        )

    for tile in range(tiles):
        weight_ref[:, tile * LANES : (tile + 1) * LANES] = scaled[tile * own : (tile + 1) * own]
    gain_ref[...] = joined(at_gain, width // LANES)
    bias = joined(at_bias, tiles)
    bias_ref[...] = bias
    row = lax.broadcasted_iota(jnp.int32, (SUBLANES, decoder), 0)
    terms = jnp.zeros((SUBLANES, decoder), jnp.float32)
    for term in range(3):
        part = bias.astype(jnp.bfloat16).astype(jnp.float32)
        terms = jnp.where(row == term, part, terms)
        bias = bias - part
    beta_ref[...] = jnp.sum(
        backproject(terms.astype(jnp.bfloat16), projection_ref), axis=0, keepdims=True
    )


VMEM = pl.BlockSpec(memory_space=pltpu.VMEM)
SMEM = pl.BlockSpec(memory_space=pltpu.SMEM)
HBM = pl.BlockSpec(memory_space=pltpu.HBM)
PARAMS = pltpu.CompilerParams(vmem_limit_bytes=32 * 1024 * 1024)


def cost(flops, transfers):
    return pl.CostEstimate(flops=flops, bytes_accessed=transfers, transcendentals=0)


def in_hbm(*arrays):
    return tuple(pltpu.with_memory_space_constraint(each, pltpu.HBM) for each in arrays)


def exchange(blocks, axis, order):
    return lax.all_to_all(blocks, axis, 0, 0, tiled=True, axis_index_groups=[order])


def make_body(dp, bal):
    def body(counts, rows, cotangent, weight, gain, beta):
        count, width = rows.shape
        decoder = cotangent.shape[1]
        half = width // CORES
        own = width // (dp * bal)
        tiles = decoder // LANES
        lines = tiles * own
        at_count = (width + decoder) // LANES
        kept = -(-(at_count + 1) // SUBLANES) * SUBLANES
        peers = dp // CORES
        gain = gain.reshape(1, width)
        beta = beta.reshape(1, width)
        work = 2 * count * width * decoder
        shape = jax.ShapeDtypeStruct
        send, hidden, normed, inv_std, weight_near = pl.pallas_call(
            prepare_kernel,
            out_shape=(
                shape((count, half + decoder), jnp.bfloat16),
                shape((count, half), jnp.bfloat16),
                shape((count, width), jnp.float32),
                shape((count, 1), jnp.float32),
                shape(weight.shape, weight.dtype),
            ),
            in_specs=[SMEM] + [HBM] * 5,
            out_specs=(VMEM,) * 5,
            scratch_shapes=[
                pltpu.VMEM(rows.shape, rows.dtype),
                pltpu.VMEM(cotangent.shape, cotangent.dtype),
                pltpu.VMEM(gain.shape, gain.dtype),
                pltpu.VMEM(beta.shape, beta.dtype),
                pltpu.SemaphoreType.DMA((5,)),
            ],
            compiler_params=PARAMS,
            cost_estimate=cost(20 * count * width, 3000000),
            name="prepare",
        )(counts, *in_hbm(rows, cotangent, weight, gain, beta))
        got = lax.ppermute(send, "bal", [(member, member ^ 1) for member in range(bal)])
        product, small, grad_rows = pl.pallas_call(
            own_kernel,
            out_shape=(
                shape((half, decoder), jnp.float32),
                shape((kept, LANES), jnp.float32),
                shape(rows.shape, rows.dtype),
            ),
            in_specs=[SMEM] + [VMEM] * 6,
            out_specs=(VMEM, VMEM, HBM),
            scratch_shapes=[
                pltpu.VMEM(rows.shape, rows.dtype),
                pltpu.SemaphoreType.DMA((count // PART_ROWS,)),
            ],
            compiler_params=PARAMS,
            cost_estimate=cost(3 * work // 2, 3000000),
            name="own",
        )(counts, hidden, normed, inv_std, send, weight_near, gain)
        first = pl.pallas_call(
            functools.partial(pair_kernel, dp, bal, own),
            out_shape=shape((bal, lines * peers + kept, LANES), jnp.bfloat16),
            in_specs=[VMEM] * 3,
            out_specs=VMEM,
            scratch_shapes=[pltpu.VMEM((tiles, (peers + 1) * (bal * own + 1), LANES), jnp.float32)],
            compiler_params=PARAMS,
            cost_estimate=cost(work // 2, 2000000),
            name="pair",
        )(got, product, small)
        first = exchange(first, "bal", bal_order(bal))
        second = pl.pallas_call(
            functools.partial(regroup_kernel, dp, lines, at_count),
            out_shape=shape((dp, lines + kept, LANES), jnp.bfloat16),
            in_specs=[VMEM],
            out_specs=VMEM,
            scratch_shapes=[pltpu.VMEM(((dp + 1) * lines, LANES), jnp.float32)],
            compiler_params=PARAMS,
            cost_estimate=cost(1000000, 1500000),
            name="regroup",
        )(first)
        second = exchange(second, "dp", dp_order(dp))
        vector = shape((1, width), jnp.float32)
        grad_weight, grad_gain, grad_beta, grad_bias = pl.pallas_call(
            finish_kernel,
            out_shape=(
                shape((own, decoder), jnp.float32),
                vector,
                vector,
                shape((1, decoder), jnp.float32),
            ),
            in_specs=[VMEM] * 2,
            out_specs=(VMEM,) * 4,
            compiler_params=PARAMS,
            cost_estimate=cost(1000000, 300000),
            name="finish",
        )(second, weight_near)
        return (
            grad_rows,
            grad_weight,
            grad_gain.reshape(width),
            grad_beta.reshape(width),
            grad_bias.reshape(decoder),
        )

    return body


def solution(mesh):
    placed = (P(("dp", "bal")), P(("dp", "bal"), None), P(("dp", "bal"), None), P(), P(), P())
    return jax.shard_map(
        make_body(mesh.shape["dp"], mesh.shape["bal"]),
        mesh=mesh,
        in_specs=placed,
        out_specs=(P(("dp", "bal"), None), P(("dp", "bal"), None), P(), P(), P()),
        check_vma=False,
    )
```

```python
import functools

import jax
import jax.numpy as jnp
from jax import lax
from jax.experimental import pallas as pl
from jax.experimental.pallas import tpu as pltpu
from jax.sharding import PartitionSpec as P

epsilon = 1e-06
LANES = 128
SUBLANES = 8
CORES = 2
PART_ROWS = 64
COUNT_BASE = 256


def ring(step, size):
    return min(step % size, -step % size)


def bal_order(bal):
    return sorted(
        range(bal), key=lambda at: (-2 * ring(at // 4, bal // 4) - at // 2 % 2 - 0.5 * (at % 2), at)
    )


def dp_order(dp):
    size_y, size_z = dp // 4, 4
    start = (size_y // 2, size_z // 2)

    def distance(at):
        return ring(at // size_z - start[0], size_y) + 2 * ring(at % size_z - start[1], size_z)

    return sorted(range(dp), key=lambda at: (distance(at), at))


def normalise(x_rows):
    x_float = x_rows.astype(jnp.float32)
    centred = x_float - jnp.mean(x_float, axis=1, keepdims=True)
    inv_std = lax.rsqrt(jnp.mean(centred * centred, axis=1, keepdims=True) + epsilon)
    return centred * inv_std, inv_std


def live_cotangent(count_ref, cot_ref):
    row = lax.broadcasted_iota(jnp.int32, cot_ref.shape, 0)
    cot = cot_ref[...]
    return jnp.where(row < count_ref[0], cot, jnp.zeros_like(cot))


def backproject(cot_live, weight_ref):
    return lax.dot_general(
        cot_live,
        weight_ref[...],
        (((1,), (1,)), ((), ())),
        preferred_element_type=jnp.float32,
    )


def project(hidden, cot_live):
    return lax.dot_general(
        hidden, cot_live, (((0,), (0,)), ((), ())), preferred_element_type=jnp.float32
    )


def start_copies(arrived, *pairs):
    copies = [
        pltpu.make_async_copy(source, target, arrived.at[index])
        for index, (source, target) in enumerate(pairs)
    ]
    for copy in copies:
        copy.start()
    return copies


def count_row(count):
    high = jnp.floor(count * (1.0 / COUNT_BASE))
    low = count - high * COUNT_BASE
    lane = lax.broadcasted_iota(jnp.int32, (1, LANES), 1)
    return jnp.where(lane == 0, high, jnp.where(lane == 1, low, 0.0))


def count_of(row):
    lane = lax.broadcasted_iota(jnp.int32, row.shape, 1)
    place = jnp.where(lane == 0, float(COUNT_BASE), jnp.where(lane == 1, 1.0, 0.0))
    return jnp.sum(row * place, axis=1, keepdims=True)


def put_lines(ref, start, vector):
    for line in range(vector.shape[1] // LANES):
        ref[start + line : start + line + 1] = vector[:, line * LANES : (line + 1) * LANES]


def prepare_kernel(
    count_ref,
    x_hbm,
    cot_hbm,
    weight_hbm,
    gain_hbm,
    beta_hbm,
    send_ref,
    hidden_ref,
    normed_ref,
    inv_std_ref,
    weight_ref,
    x_ref,
    cot_ref,
    gain_ref,
    beta_ref,
    arrived,
):
    half = hidden_ref.shape[1]
    copies = start_copies(
        arrived,
        (x_hbm, x_ref),
        (gain_hbm, gain_ref),
        (beta_hbm, beta_ref),
        (cot_hbm, cot_ref),
        (weight_hbm, weight_ref),
    )
    first_core = lax.axis_index("bal") % CORES == 0
    copies[0].wait()
    normed, inv_std = normalise(x_ref[...])
    normed_ref[...] = normed
    inv_std_ref[...] = inv_std
    for copy in copies[1:3]:
        copy.wait()
    hidden = (normed * gain_ref[...] + beta_ref[...]).astype(jnp.bfloat16)
    low, high = hidden[:, :half], hidden[:, half:]
    hidden_ref[...] = jnp.where(first_core, low, high)
    send_ref[:, :half] = jnp.where(first_core, high, low)
    copies[3].wait()
    send_ref[:, half:] = live_cotangent(count_ref, cot_ref)
    copies[4].wait()


def own_kernel(
    count_ref,
    hidden_ref,
    normed_ref,
    inv_std_ref,
    send_ref,
    weight_ref,
    gain_ref,
    product_ref,
    small,
    rows_hbm,
    rows_ref,
    left,
):
    width, decoder = weight_ref.shape
    cot_live = send_ref[:, hidden_ref.shape[1] :]
    grad_h = backproject(cot_live, weight_ref)
    count = rows_ref.shape[0]
    copies = []
    for start in range(0, count, PART_ROWS):
        part = slice(start, start + PART_ROWS)
        normed = normed_ref[part]
        scaled = grad_h[part] * gain_ref[...]
        rows_ref[part] = (
            inv_std_ref[part]
            * (
                scaled
                - jnp.mean(scaled, axis=1, keepdims=True)
                - normed * jnp.mean(scaled * normed, axis=1, keepdims=True)
            )
        ).astype(jnp.bfloat16)
        copies.append(
            pltpu.make_async_copy(
                rows_ref.at[part], rows_hbm.at[part], left.at[start // PART_ROWS]
            )
        )
        copies[-1].start()
    grad_gain = jnp.sum(grad_h * normed_ref[...], axis=0, keepdims=True)
    grad_bias = jnp.sum(cot_live.astype(jnp.float32), axis=0, keepdims=True)
    small[...] = jnp.zeros_like(small)
    put_lines(small, 0, grad_gain)
    put_lines(small, width // LANES, grad_bias)
    at = (width + decoder) // LANES
    small[at : at + 1] = count_row(
        jnp.full((1, 1), count_ref[0], jnp.int32).astype(jnp.float32)
    )
    product_ref[...] = project(hidden_ref[...], cot_live)
    for copy in copies:
        copy.wait()


def pair_kernel(dp, bal, own, got_ref, product_ref, small_ref, out_ref, grad_w):
    span = bal * own
    pitch = span + 1
    peers = dp // CORES
    half, decoder = product_ref.shape
    product = product_ref[...] + project(got_ref[:, :half], got_ref[:, half:])
    for tile in range(decoder // LANES):
        at = slice(tile * LANES, (tile + 1) * LANES)
        for peer in range(peers):
            grad_w[tile, peer * pitch : peer * pitch + span] = product[
                peer * span : (peer + 1) * span, at
            ]
    small = small_ref[...].astype(jnp.bfloat16)
    tiles = decoder // LANES
    for place, owner in enumerate(bal_order(bal)):
        for tile in range(tiles):
            for row in range(own):
                rows = pl.ds(owner * own + row, peers, stride=pitch)
                at = (tile * own + row) * peers
                out_ref[place, at : at + peers, :] = grad_w[tile, rows, :].astype(jnp.bfloat16)
        out_ref[place, tiles * own * peers :, :] = small


def regroup_kernel(dp, lines, at_count, got_ref, out_ref, spread):
    bal = got_ref.shape[0]
    peers = dp // CORES
    halves = [0.0] * CORES
    for place, member in enumerate(bal_order(bal)):
        halves[member % CORES] += got_ref[place].astype(jnp.float32)
    small = sum(part[lines * peers :] for part in halves)
    line = lax.broadcasted_iota(jnp.int32, small.shape, 0)
    count = count_of(small[at_count : at_count + 1])
    small = jnp.where(line == at_count, count_row(count), small)
    for core in range(CORES):
        for row in range(lines):
            spread[pl.ds(core * peers * lines + row, peers, stride=lines), :] = halves[core][
                row * peers : (row + 1) * peers
            ]
    for place, peer in enumerate(dp_order(dp)):
        block = [spread[peer * lines : (peer + 1) * lines], small]
        out_ref[place] = jnp.concatenate(block, axis=0).astype(jnp.bfloat16)


def finish_kernel(got_ref, projection_ref, weight_ref, gain_ref, beta_ref, bias_ref):
    width, decoder = projection_ref.shape
    own, tiles = weight_ref.shape[0], decoder // LANES
    total = jnp.sum(got_ref[...].astype(jnp.float32), axis=0)
    at_gain = own * tiles
    at_bias = at_gain + width // LANES
    at_count = at_bias + tiles

    def joined(start, lines):
        return jnp.concatenate(
            [total[start + line : start + line + 1] for line in range(lines)], axis=1
        )

    bias = joined(at_bias, tiles)
    rest = bias
    row = lax.broadcasted_iota(jnp.int32, (SUBLANES, decoder), 0)
    terms = jnp.zeros((SUBLANES, decoder), jnp.float32)
    for term in range(3):
        part = rest.astype(jnp.bfloat16).astype(jnp.float32)
        terms = jnp.where(row == term, part, terms)
        rest = rest - part
    beta = backproject(terms.astype(jnp.bfloat16), projection_ref)
    scale = lax.rsqrt(count_of(total[at_count : at_count + 1]))
    for tile in range(tiles):
        weight_ref[:, tile * LANES : (tile + 1) * LANES] = (
            total[tile * own : (tile + 1) * own] * scale
        )
    gain_ref[...] = joined(at_gain, width // LANES) * scale
    bias_ref[...] = bias * scale
    beta_ref[...] = jnp.sum(beta, axis=0, keepdims=True) * scale


VMEM = pl.BlockSpec(memory_space=pltpu.VMEM)
SMEM = pl.BlockSpec(memory_space=pltpu.SMEM)
HBM = pl.BlockSpec(memory_space=pltpu.HBM)
PARAMS = pltpu.CompilerParams(vmem_limit_bytes=32 * 1024 * 1024)


def cost(flops, transfers):
    return pl.CostEstimate(flops=flops, bytes_accessed=transfers, transcendentals=0)


def in_hbm(*arrays):
    return tuple(pltpu.with_memory_space_constraint(each, pltpu.HBM) for each in arrays)


def exchange(blocks, axis, order):
    return lax.all_to_all(blocks, axis, 0, 0, tiled=True, axis_index_groups=[order])


def make_body(dp, bal):
    def body(counts, rows, cotangent, weight, gain, beta):
        count, width = rows.shape
        decoder = cotangent.shape[1]
        half = width // CORES
        own = width // (dp * bal)
        tiles = decoder // LANES
        lines = tiles * own
        at_count = (width + decoder) // LANES
        kept = -(-(at_count + 1) // SUBLANES) * SUBLANES
        peers = dp // CORES
        gain = gain.reshape(1, width)
        beta = beta.reshape(1, width)
        work = 2 * count * width * decoder
        shape = jax.ShapeDtypeStruct
        send, hidden, normed, inv_std, weight_near = pl.pallas_call(
            prepare_kernel,
            out_shape=(
                shape((count, half + decoder), jnp.bfloat16),
                shape((count, half), jnp.bfloat16),
                shape((count, width), jnp.float32),
                shape((count, 1), jnp.float32),
                shape(weight.shape, weight.dtype),
            ),
            in_specs=[SMEM] + [HBM] * 5,
            out_specs=(VMEM,) * 5,
            scratch_shapes=[
                pltpu.VMEM(rows.shape, rows.dtype),
                pltpu.VMEM(cotangent.shape, cotangent.dtype),
                pltpu.VMEM(gain.shape, gain.dtype),
                pltpu.VMEM(beta.shape, beta.dtype),
                pltpu.SemaphoreType.DMA((5,)),
            ],
            compiler_params=PARAMS,
            cost_estimate=cost(20 * count * width, 3000000),
            name="prepare",
        )(counts, *in_hbm(rows, cotangent, weight, gain, beta))
        got = lax.ppermute(send, "bal", [(member, member ^ 1) for member in range(bal)])
        product, small, grad_rows = pl.pallas_call(
            own_kernel,
            out_shape=(
                shape((half, decoder), jnp.float32),
                shape((kept, LANES), jnp.float32),
                shape(rows.shape, rows.dtype),
            ),
            in_specs=[SMEM] + [VMEM] * 6,
            out_specs=(VMEM, VMEM, HBM),
            scratch_shapes=[
                pltpu.VMEM(rows.shape, rows.dtype),
                pltpu.SemaphoreType.DMA((count // PART_ROWS,)),
            ],
            compiler_params=PARAMS,
            cost_estimate=cost(3 * work // 2, 3000000),
            name="own",
        )(counts, hidden, normed, inv_std, send, weight_near, gain)
        first = pl.pallas_call(
            functools.partial(pair_kernel, dp, bal, own),
            out_shape=shape((bal, lines * peers + kept, LANES), jnp.bfloat16),
            in_specs=[VMEM] * 3,
            out_specs=VMEM,
            scratch_shapes=[pltpu.VMEM((tiles, (peers + 1) * (bal * own + 1), LANES), jnp.float32)],
            compiler_params=PARAMS,
            cost_estimate=cost(work // 2, 2000000),
            name="pair",
        )(got, product, small)
        first = exchange(first, "bal", bal_order(bal))
        second = pl.pallas_call(
            functools.partial(regroup_kernel, dp, lines, at_count),
            out_shape=shape((dp, lines + kept, LANES), jnp.bfloat16),
            in_specs=[VMEM],
            out_specs=VMEM,
            scratch_shapes=[pltpu.VMEM(((dp + 1) * lines, LANES), jnp.float32)],
            compiler_params=PARAMS,
            cost_estimate=cost(1000000, 1500000),
            name="regroup",
        )(first)
        second = exchange(second, "dp", dp_order(dp))
        vector = shape((1, width), jnp.float32)
        grad_weight, grad_gain, grad_beta, grad_bias = pl.pallas_call(
            finish_kernel,
            out_shape=(
                shape((own, decoder), jnp.float32),
                vector,
                vector,
                shape((1, decoder), jnp.float32),
            ),
            in_specs=[VMEM] * 2,
            out_specs=(VMEM,) * 4,
            compiler_params=PARAMS,
            cost_estimate=cost(1000000, 300000),
            name="finish",
        )(second, weight_near)
        return (
            grad_rows,
            grad_weight,
            grad_gain.reshape(width),
            grad_beta.reshape(width),
            grad_bias.reshape(decoder),
        )

    return body


def solution(mesh):
    placed = (P(("dp", "bal")), P(("dp", "bal"), None), P(("dp", "bal"), None), P(), P(), P())
    return jax.shard_map(
        make_body(mesh.shape["dp"], mesh.shape["bal"]),
        mesh=mesh,
        in_specs=placed,
        out_specs=(P(("dp", "bal"), None), P(("dp", "bal"), None), P(), P(), P()),
        check_vma=False,
    )
```

```python
import functools

import jax
import jax.numpy as jnp
from jax import lax
from jax.experimental import pallas as pl
from jax.experimental.pallas import tpu as pltpu
from jax.sharding import PartitionSpec as P

epsilon = 1e-06
LANES = 128
SUBLANES = 8
CORES = 2
PART_ROWS = 64
COUNT_BASE = 256


def bal_order(bal):
    far = 3 * bal // 4 - 1
    return [far] + [at for at in range(bal) if at != far]


def dp_order(dp):
    far = dp // 2 + 2
    return [far] + [at for at in range(dp) if at != far]


def normalise(x_rows):
    x_float = x_rows.astype(jnp.float32)
    centred = x_float - jnp.mean(x_float, axis=1, keepdims=True)
    inv_std = lax.rsqrt(jnp.mean(centred * centred, axis=1, keepdims=True) + epsilon)
    return centred * inv_std, inv_std


def live_cotangent(count_ref, cot_ref):
    row = lax.broadcasted_iota(jnp.int32, cot_ref.shape, 0)
    cot = cot_ref[...]
    return jnp.where(row < count_ref[0], cot, jnp.zeros_like(cot))


def backproject(cot_live, weight_ref):
    return lax.dot_general(
        cot_live,
        weight_ref[...],
        (((1,), (1,)), ((), ())),
        preferred_element_type=jnp.float32,
    )


def project(hidden, cot_live):
    return lax.dot_general(
        hidden, cot_live, (((0,), (0,)), ((), ())), preferred_element_type=jnp.float32
    )


def start_copies(arrived, *pairs):
    copies = [
        pltpu.make_async_copy(source, target, arrived.at[index])
        for index, (source, target) in enumerate(pairs)
    ]
    for copy in copies:
        copy.start()
    return copies


def count_row(count):
    high = jnp.floor(count * (1.0 / COUNT_BASE))
    low = count - high * COUNT_BASE
    lane = lax.broadcasted_iota(jnp.int32, (1, LANES), 1)
    return jnp.where(lane == 0, high, jnp.where(lane == 1, low, 0.0))


def count_of(row):
    lane = lax.broadcasted_iota(jnp.int32, row.shape, 1)
    place = jnp.where(lane == 0, float(COUNT_BASE), jnp.where(lane == 1, 1.0, 0.0))
    return jnp.sum(row * place, axis=1, keepdims=True)


def put_lines(ref, start, vector):
    for line in range(vector.shape[1] // LANES):
        ref[start + line : start + line + 1] = vector[:, line * LANES : (line + 1) * LANES]


def prepare_kernel(
    count_ref,
    x_hbm,
    cot_hbm,
    weight_hbm,
    gain_hbm,
    beta_hbm,
    send_ref,
    hidden_ref,
    normed_ref,
    inv_std_ref,
    weight_ref,
    x_ref,
    cot_ref,
    gain_ref,
    beta_ref,
    arrived,
):
    half = hidden_ref.shape[1]
    copies = start_copies(
        arrived,
        (cot_hbm, cot_ref),
        (x_hbm, x_ref),
        (gain_hbm, gain_ref),
        (beta_hbm, beta_ref),
        (weight_hbm, weight_ref),
    )
    first_core = lax.axis_index("bal") % CORES == 0
    copies[0].wait()
    send_ref[:, half:] = live_cotangent(count_ref, cot_ref)
    copies[1].wait()
    normed, inv_std = normalise(x_ref[...])
    normed_ref[...] = normed
    inv_std_ref[...] = inv_std
    for copy in copies[2:4]:
        copy.wait()
    hidden = (normed * gain_ref[...] + beta_ref[...]).astype(jnp.bfloat16)
    low, high = hidden[:, :half], hidden[:, half:]
    hidden_ref[...] = jnp.where(first_core, low, high)
    send_ref[:, :half] = jnp.where(first_core, high, low)
    copies[4].wait()


def own_kernel(
    count_ref,
    hidden_ref,
    normed_ref,
    inv_std_ref,
    send_ref,
    weight_ref,
    gain_ref,
    product_ref,
    small,
    rows_hbm,
    rows_ref,
    left,
):
    width, decoder = weight_ref.shape
    cot_live = send_ref[:, hidden_ref.shape[1] :]
    grad_h = backproject(cot_live, weight_ref)
    count = rows_ref.shape[0]
    copies = []
    for start in range(0, count, PART_ROWS):
        part = slice(start, start + PART_ROWS)
        normed = normed_ref[part]
        scaled = grad_h[part] * gain_ref[...]
        rows_ref[part] = (
            inv_std_ref[part]
            * (
                scaled
                - jnp.mean(scaled, axis=1, keepdims=True)
                - normed * jnp.mean(scaled * normed, axis=1, keepdims=True)
            )
        ).astype(jnp.bfloat16)
        copies.append(
            pltpu.make_async_copy(
                rows_ref.at[part], rows_hbm.at[part], left.at[start // PART_ROWS]
            )
        )
        copies[-1].start()
    grad_gain = jnp.sum(grad_h * normed_ref[...], axis=0, keepdims=True)
    grad_bias = jnp.sum(cot_live.astype(jnp.float32), axis=0, keepdims=True)
    small[...] = jnp.zeros_like(small)
    put_lines(small, 0, grad_gain)
    put_lines(small, width // LANES, grad_bias)
    at = (width + decoder) // LANES
    small[at : at + 1] = count_row(
        jnp.full((1, 1), count_ref[0], jnp.int32).astype(jnp.float32)
    )
    product_ref[...] = project(hidden_ref[...], cot_live)
    for copy in copies:
        copy.wait()


def pair_kernel(dp, bal, own, got_ref, product_ref, small_ref, out_ref, grad_w):
    span = bal * own
    pitch = span + 1
    peers = dp // CORES
    half, decoder = product_ref.shape
    product = product_ref[...] + project(got_ref[:, :half], got_ref[:, half:])
    for tile in range(decoder // LANES):
        at = slice(tile * LANES, (tile + 1) * LANES)
        for peer in range(peers):
            grad_w[tile, peer * pitch : peer * pitch + span] = product[
                peer * span : (peer + 1) * span, at
            ]
    small = small_ref[...].astype(jnp.bfloat16)
    tiles = decoder // LANES
    for place, owner in enumerate(bal_order(bal)):
        for tile in range(tiles):
            for row in range(own):
                rows = pl.ds(owner * own + row, peers, stride=pitch)
                at = (tile * own + row) * peers
                out_ref[place, at : at + peers, :] = grad_w[tile, rows, :].astype(jnp.bfloat16)
        out_ref[place, tiles * own * peers :, :] = small


def regroup_kernel(dp, lines, at_count, got_ref, out_ref, spread):
    bal = got_ref.shape[0]
    peers = dp // CORES
    halves = [0.0] * CORES
    for place, member in enumerate(bal_order(bal)):
        halves[member % CORES] += got_ref[place].astype(jnp.float32)
    small = sum(part[lines * peers :] for part in halves)
    line = lax.broadcasted_iota(jnp.int32, small.shape, 0)
    count = count_of(small[at_count : at_count + 1])
    small = jnp.where(line == at_count, count_row(count), small)
    for core in range(CORES):
        for row in range(lines):
            spread[pl.ds(core * peers * lines + row, peers, stride=lines), :] = halves[core][
                row * peers : (row + 1) * peers
            ]
    for place, peer in enumerate(dp_order(dp)):
        block = [spread[peer * lines : (peer + 1) * lines], small]
        out_ref[place] = jnp.concatenate(block, axis=0).astype(jnp.bfloat16)


def finish_kernel(got_ref, projection_ref, weight_ref, gain_ref, beta_ref, bias_ref):
    width, decoder = projection_ref.shape
    own, tiles = weight_ref.shape[0], decoder // LANES
    total = jnp.sum(got_ref[...].astype(jnp.float32), axis=0)
    at_gain = own * tiles
    at_bias = at_gain + width // LANES
    at_count = at_bias + tiles

    def joined(start, lines):
        return jnp.concatenate(
            [total[start + line : start + line + 1] for line in range(lines)], axis=1
        )

    bias = joined(at_bias, tiles)
    rest = bias
    row = lax.broadcasted_iota(jnp.int32, (SUBLANES, decoder), 0)
    terms = jnp.zeros((SUBLANES, decoder), jnp.float32)
    for term in range(3):
        part = rest.astype(jnp.bfloat16).astype(jnp.float32)
        terms = jnp.where(row == term, part, terms)
        rest = rest - part
    beta = backproject(terms.astype(jnp.bfloat16), projection_ref)
    scale = lax.rsqrt(count_of(total[at_count : at_count + 1]))
    for tile in range(tiles):
        weight_ref[:, tile * LANES : (tile + 1) * LANES] = (
            total[tile * own : (tile + 1) * own] * scale
        )
    gain_ref[...] = joined(at_gain, width // LANES) * scale
    bias_ref[...] = bias * scale
    beta_ref[...] = jnp.sum(beta, axis=0, keepdims=True) * scale


VMEM = pl.BlockSpec(memory_space=pltpu.VMEM)
SMEM = pl.BlockSpec(memory_space=pltpu.SMEM)
HBM = pl.BlockSpec(memory_space=pltpu.HBM)
PARAMS = pltpu.CompilerParams(vmem_limit_bytes=32 * 1024 * 1024)


def cost(flops, transfers):
    return pl.CostEstimate(flops=flops, bytes_accessed=transfers, transcendentals=0)


def in_hbm(*arrays):
    return tuple(pltpu.with_memory_space_constraint(each, pltpu.HBM) for each in arrays)


def exchange(blocks, axis, order):
    return lax.all_to_all(blocks, axis, 0, 0, tiled=True, axis_index_groups=[order])


def make_body(dp, bal):
    def body(counts, rows, cotangent, weight, gain, beta):
        count, width = rows.shape
        decoder = cotangent.shape[1]
        half = width // CORES
        own = width // (dp * bal)
        tiles = decoder // LANES
        lines = tiles * own
        at_count = (width + decoder) // LANES
        kept = -(-(at_count + 1) // SUBLANES) * SUBLANES
        peers = dp // CORES
        gain = gain.reshape(1, width)
        beta = beta.reshape(1, width)
        work = 2 * count * width * decoder
        shape = jax.ShapeDtypeStruct
        send, hidden, normed, inv_std, weight_near = pl.pallas_call(
            prepare_kernel,
            out_shape=(
                shape((count, half + decoder), jnp.bfloat16),
                shape((count, half), jnp.bfloat16),
                shape((count, width), jnp.float32),
                shape((count, 1), jnp.float32),
                shape(weight.shape, weight.dtype),
            ),
            in_specs=[SMEM] + [HBM] * 5,
            out_specs=(VMEM,) * 5,
            scratch_shapes=[
                pltpu.VMEM(rows.shape, rows.dtype),
                pltpu.VMEM(cotangent.shape, cotangent.dtype),
                pltpu.VMEM(gain.shape, gain.dtype),
                pltpu.VMEM(beta.shape, beta.dtype),
                pltpu.SemaphoreType.DMA((5,)),
            ],
            compiler_params=PARAMS,
            cost_estimate=cost(20 * count * width, 3000000),
            name="prepare",
        )(counts, *in_hbm(rows, cotangent, weight, gain, beta))
        got = lax.ppermute(send, "bal", [(member, member ^ 1) for member in range(bal)])
        product, small, grad_rows = pl.pallas_call(
            own_kernel,
            out_shape=(
                shape((half, decoder), jnp.float32),
                shape((kept, LANES), jnp.float32),
                shape(rows.shape, rows.dtype),
            ),
            in_specs=[SMEM] + [VMEM] * 6,
            out_specs=(VMEM, VMEM, HBM),
            scratch_shapes=[
                pltpu.VMEM(rows.shape, rows.dtype),
                pltpu.SemaphoreType.DMA((count // PART_ROWS,)),
            ],
            compiler_params=PARAMS,
            cost_estimate=cost(3 * work // 2, 3000000),
            name="own",
        )(counts, hidden, normed, inv_std, send, weight_near, gain)
        first = pl.pallas_call(
            functools.partial(pair_kernel, dp, bal, own),
            out_shape=shape((bal, lines * peers + kept, LANES), jnp.bfloat16),
            in_specs=[VMEM] * 3,
            out_specs=VMEM,
            scratch_shapes=[pltpu.VMEM((tiles, (peers + 1) * (bal * own + 1), LANES), jnp.float32)],
            compiler_params=PARAMS,
            cost_estimate=cost(work // 2, 2000000),
            name="pair",
        )(got, product, small)
        first = exchange(first, "bal", bal_order(bal))
        second = pl.pallas_call(
            functools.partial(regroup_kernel, dp, lines, at_count),
            out_shape=shape((dp, lines + kept, LANES), jnp.bfloat16),
            in_specs=[VMEM],
            out_specs=VMEM,
            scratch_shapes=[pltpu.VMEM(((dp + 1) * lines, LANES), jnp.float32)],
            compiler_params=PARAMS,
            cost_estimate=cost(1000000, 1500000),
            name="regroup",
        )(first)
        second = exchange(second, "dp", dp_order(dp))
        vector = shape((1, width), jnp.float32)
        grad_weight, grad_gain, grad_beta, grad_bias = pl.pallas_call(
            finish_kernel,
            out_shape=(
                shape((own, decoder), jnp.float32),
                vector,
                vector,
                shape((1, decoder), jnp.float32),
            ),
            in_specs=[VMEM] * 2,
            out_specs=(VMEM,) * 4,
            compiler_params=PARAMS,
            cost_estimate=cost(1000000, 300000),
            name="finish",
        )(second, weight_near)
        return (
            grad_rows,
            grad_weight,
            grad_gain.reshape(width),
            grad_beta.reshape(width),
            grad_bias.reshape(decoder),
        )

    return body


def solution(mesh):
    placed = (P(("dp", "bal")), P(("dp", "bal"), None), P(("dp", "bal"), None), P(), P(), P())
    return jax.shard_map(
        make_body(mesh.shape["dp"], mesh.shape["bal"]),
        mesh=mesh,
        in_specs=placed,
        out_specs=(P(("dp", "bal"), None), P(("dp", "bal"), None), P(), P(), P()),
        check_vma=False,
    )
```

```python
import functools

import jax
import jax.numpy as jnp
from jax import lax
from jax.experimental import pallas as pl
from jax.experimental.pallas import tpu as pltpu
from jax.sharding import PartitionSpec as P

epsilon = 1e-06
LANES = 128
SUBLANES = 8
CORES = 2
PART_ROWS = 64
COUNT_BASE = 256


def bal_order(bal):
    far = 3 * bal // 4 - 1
    return [far] + [at for at in range(bal) if at != far]


def dp_order(dp):
    far = dp // 2 + 2
    return [far] + [at for at in range(dp) if at != far]


def normalise(x_rows):
    x_float = x_rows.astype(jnp.float32)
    centred = x_float - jnp.mean(x_float, axis=1, keepdims=True)
    inv_std = lax.rsqrt(jnp.mean(centred * centred, axis=1, keepdims=True) + epsilon)
    return centred * inv_std, inv_std


def live_cotangent(count_ref, cot_ref):
    row = lax.broadcasted_iota(jnp.int32, cot_ref.shape, 0)
    cot = cot_ref[...]
    return jnp.where(row < count_ref[0], cot, jnp.zeros_like(cot))


def backproject(cot_live, weight_ref):
    return lax.dot_general(
        cot_live,
        weight_ref[...],
        (((1,), (1,)), ((), ())),
        preferred_element_type=jnp.float32,
    )


def project(hidden, cot_live):
    return lax.dot_general(
        hidden, cot_live, (((0,), (0,)), ((), ())), preferred_element_type=jnp.float32
    )


def start_copies(arrived, *pairs):
    copies = [
        pltpu.make_async_copy(source, target, arrived.at[index])
        for index, (source, target) in enumerate(pairs)
    ]
    for copy in copies:
        copy.start()
    return copies


def count_row(count):
    high = jnp.floor(count * (1.0 / COUNT_BASE))
    low = count - high * COUNT_BASE
    lane = lax.broadcasted_iota(jnp.int32, (1, LANES), 1)
    return jnp.where(lane == 0, high, jnp.where(lane == 1, low, 0.0))


def count_of(row):
    lane = lax.broadcasted_iota(jnp.int32, row.shape, 1)
    place = jnp.where(lane == 0, float(COUNT_BASE), jnp.where(lane == 1, 1.0, 0.0))
    return jnp.sum(row * place, axis=1, keepdims=True)


def put_lines(ref, start, vector):
    for line in range(vector.shape[1] // LANES):
        ref[start + line : start + line + 1] = vector[:, line * LANES : (line + 1) * LANES]


def prepare_kernel(
    count_ref,
    x_hbm,
    cot_hbm,
    weight_hbm,
    gain_hbm,
    beta_hbm,
    send_ref,
    hidden_ref,
    normed_ref,
    inv_std_ref,
    weight_ref,
    x_ref,
    cot_ref,
    gain_ref,
    beta_ref,
    arrived,
):
    half = hidden_ref.shape[1]
    copies = start_copies(
        arrived,
        (cot_hbm, cot_ref),
        (x_hbm, x_ref),
        (gain_hbm, gain_ref),
        (beta_hbm, beta_ref),
        (weight_hbm, weight_ref),
    )
    first_core = lax.axis_index("bal") % CORES == 0
    copies[0].wait()
    send_ref[:, half:] = live_cotangent(count_ref, cot_ref)
    copies[1].wait()
    normed, inv_std = normalise(x_ref[...])
    normed_ref[...] = normed
    inv_std_ref[...] = inv_std
    for copy in copies[2:4]:
        copy.wait()
    hidden = (normed * gain_ref[...] + beta_ref[...]).astype(jnp.bfloat16)
    low, high = hidden[:, :half], hidden[:, half:]
    hidden_ref[...] = jnp.where(first_core, low, high)
    send_ref[:, :half] = jnp.where(first_core, high, low)
    copies[4].wait()


def own_kernel(
    count_ref,
    hidden_ref,
    normed_ref,
    inv_std_ref,
    send_ref,
    weight_ref,
    gain_ref,
    product_ref,
    small,
    rows_hbm,
    rows_ref,
    left,
):
    width, decoder = weight_ref.shape
    cot_live = send_ref[:, hidden_ref.shape[1] :]
    grad_h = backproject(cot_live, weight_ref)
    count = rows_ref.shape[0]
    copies = []
    for start in range(0, count, PART_ROWS):
        part = slice(start, start + PART_ROWS)
        normed = normed_ref[part]
        scaled = grad_h[part] * gain_ref[...]
        rows_ref[part] = (
            inv_std_ref[part]
            * (
                scaled
                - jnp.mean(scaled, axis=1, keepdims=True)
                - normed * jnp.mean(scaled * normed, axis=1, keepdims=True)
            )
        ).astype(jnp.bfloat16)
        copies.append(
            pltpu.make_async_copy(
                rows_ref.at[part], rows_hbm.at[part], left.at[start // PART_ROWS]
            )
        )
        copies[-1].start()
    grad_gain = jnp.sum(grad_h * normed_ref[...], axis=0, keepdims=True)
    grad_bias = jnp.sum(cot_live.astype(jnp.float32), axis=0, keepdims=True)
    small[...] = jnp.zeros_like(small)
    put_lines(small, 0, grad_gain)
    put_lines(small, width // LANES, grad_bias)
    at = (width + decoder) // LANES
    small[at : at + 1] = count_row(
        jnp.full((1, 1), count_ref[0], jnp.int32).astype(jnp.float32)
    )
    product_ref[...] = project(hidden_ref[...], cot_live)
    for copy in copies:
        copy.wait()


def pair_kernel(dp, bal, own, got_ref, product_ref, small_ref, out_ref, grad_w):
    span = bal * own
    pitch = span + 1
    peers = dp // CORES
    half, decoder = product_ref.shape
    tiles = decoder // LANES
    small = small_ref[...].astype(jnp.bfloat16)
    order = bal_order(bal)
    for place in range(bal):
        out_ref[place, tiles * own * peers :, :] = small
    hidden = got_ref[:, :half]
    for first in range(0, tiles, 2):
        at = slice(first * LANES, (first + 2) * LANES)
        cot_live = got_ref[:, half + first * LANES : half + (first + 2) * LANES]
        product = product_ref[:, at] + project(hidden, cot_live)
        for tile in (first, first + 1):
            at = slice((tile - first) * LANES, (tile - first + 1) * LANES)
            for peer in range(peers):
                grad_w[tile, peer * pitch : peer * pitch + span] = product[
                    peer * span : (peer + 1) * span, at
                ]
            for place, owner in enumerate(order):
                for row in range(own):
                    rows = pl.ds(owner * own + row, peers, stride=pitch)
                    at_row = (tile * own + row) * peers
                    out_ref[place, at_row : at_row + peers, :] = grad_w[tile, rows, :].astype(
                        jnp.bfloat16
                    )


def regroup_kernel(dp, lines, at_count, got_ref, out_ref, spread):
    bal = got_ref.shape[0]
    peers = dp // CORES
    halves = [0.0] * CORES
    for place, member in enumerate(bal_order(bal)):
        halves[member % CORES] += got_ref[place].astype(jnp.float32)
    small = sum(part[lines * peers :] for part in halves)
    line = lax.broadcasted_iota(jnp.int32, small.shape, 0)
    count = count_of(small[at_count : at_count + 1])
    small = jnp.where(line == at_count, count_row(count), small)
    for core in range(CORES):
        for row in range(lines):
            spread[pl.ds(core * peers * lines + row, peers, stride=lines), :] = halves[core][
                row * peers : (row + 1) * peers
            ]
    for place, peer in enumerate(dp_order(dp)):
        block = [spread[peer * lines : (peer + 1) * lines], small]
        out_ref[place] = jnp.concatenate(block, axis=0).astype(jnp.bfloat16)


def finish_kernel(got_ref, projection_ref, weight_ref, gain_ref, beta_ref, bias_ref):
    width, decoder = projection_ref.shape
    own, tiles = weight_ref.shape[0], decoder // LANES
    total = jnp.sum(got_ref[...].astype(jnp.float32), axis=0)
    at_gain = own * tiles
    at_bias = at_gain + width // LANES
    at_count = at_bias + tiles

    def joined(start, lines):
        return jnp.concatenate(
            [total[start + line : start + line + 1] for line in range(lines)], axis=1
        )

    bias = joined(at_bias, tiles)
    rest = bias
    row = lax.broadcasted_iota(jnp.int32, (SUBLANES, decoder), 0)
    terms = jnp.zeros((SUBLANES, decoder), jnp.float32)
    for term in range(3):
        part = rest.astype(jnp.bfloat16).astype(jnp.float32)
        terms = jnp.where(row == term, part, terms)
        rest = rest - part
    beta = backproject(terms.astype(jnp.bfloat16), projection_ref)
    scale = lax.rsqrt(count_of(total[at_count : at_count + 1]))
    for tile in range(tiles):
        weight_ref[:, tile * LANES : (tile + 1) * LANES] = (
            total[tile * own : (tile + 1) * own] * scale
        )
    gain_ref[...] = joined(at_gain, width // LANES) * scale
    bias_ref[...] = bias * scale
    beta_ref[...] = jnp.sum(beta, axis=0, keepdims=True) * scale


VMEM = pl.BlockSpec(memory_space=pltpu.VMEM)
SMEM = pl.BlockSpec(memory_space=pltpu.SMEM)
HBM = pl.BlockSpec(memory_space=pltpu.HBM)
PARAMS = pltpu.CompilerParams(vmem_limit_bytes=32 * 1024 * 1024)


def cost(flops, transfers):
    return pl.CostEstimate(flops=flops, bytes_accessed=transfers, transcendentals=0)


def in_hbm(*arrays):
    return tuple(pltpu.with_memory_space_constraint(each, pltpu.HBM) for each in arrays)


def exchange(blocks, axis, order):
    return lax.all_to_all(blocks, axis, 0, 0, tiled=True, axis_index_groups=[order])


def make_body(dp, bal):
    def body(counts, rows, cotangent, weight, gain, beta):
        count, width = rows.shape
        decoder = cotangent.shape[1]
        half = width // CORES
        own = width // (dp * bal)
        tiles = decoder // LANES
        lines = tiles * own
        at_count = (width + decoder) // LANES
        kept = -(-(at_count + 1) // SUBLANES) * SUBLANES
        peers = dp // CORES
        gain = gain.reshape(1, width)
        beta = beta.reshape(1, width)
        work = 2 * count * width * decoder
        shape = jax.ShapeDtypeStruct
        send, hidden, normed, inv_std, weight_near = pl.pallas_call(
            prepare_kernel,
            out_shape=(
                shape((count, half + decoder), jnp.bfloat16),
                shape((count, half), jnp.bfloat16),
                shape((count, width), jnp.float32),
                shape((count, 1), jnp.float32),
                shape(weight.shape, weight.dtype),
            ),
            in_specs=[SMEM] + [HBM] * 5,
            out_specs=(VMEM,) * 5,
            scratch_shapes=[
                pltpu.VMEM(rows.shape, rows.dtype),
                pltpu.VMEM(cotangent.shape, cotangent.dtype),
                pltpu.VMEM(gain.shape, gain.dtype),
                pltpu.VMEM(beta.shape, beta.dtype),
                pltpu.SemaphoreType.DMA((5,)),
            ],
            compiler_params=PARAMS,
            cost_estimate=cost(20 * count * width, 3000000),
            name="prepare",
        )(counts, *in_hbm(rows, cotangent, weight, gain, beta))
        got = lax.ppermute(send, "bal", [(member, member ^ 1) for member in range(bal)])
        product, small, grad_rows = pl.pallas_call(
            own_kernel,
            out_shape=(
                shape((half, decoder), jnp.float32),
                shape((kept, LANES), jnp.float32),
                shape(rows.shape, rows.dtype),
            ),
            in_specs=[SMEM] + [VMEM] * 6,
            out_specs=(VMEM, VMEM, HBM),
            scratch_shapes=[
                pltpu.VMEM(rows.shape, rows.dtype),
                pltpu.SemaphoreType.DMA((count // PART_ROWS,)),
            ],
            compiler_params=PARAMS,
            cost_estimate=cost(3 * work // 2, 3000000),
            name="own",
        )(counts, hidden, normed, inv_std, send, weight_near, gain)
        first = pl.pallas_call(
            functools.partial(pair_kernel, dp, bal, own),
            out_shape=shape((bal, lines * peers + kept, LANES), jnp.bfloat16),
            in_specs=[VMEM] * 3,
            out_specs=VMEM,
            scratch_shapes=[pltpu.VMEM((tiles, (peers + 1) * (bal * own + 1), LANES), jnp.float32)],
            compiler_params=PARAMS,
            cost_estimate=cost(work // 2, 2000000),
            name="pair",
        )(got, product, small)
        first = exchange(first, "bal", bal_order(bal))
        second = pl.pallas_call(
            functools.partial(regroup_kernel, dp, lines, at_count),
            out_shape=shape((dp, lines + kept, LANES), jnp.bfloat16),
            in_specs=[VMEM],
            out_specs=VMEM,
            scratch_shapes=[pltpu.VMEM(((dp + 1) * lines, LANES), jnp.float32)],
            compiler_params=PARAMS,
            cost_estimate=cost(1000000, 1500000),
            name="regroup",
        )(first)
        second = exchange(second, "dp", dp_order(dp))
        vector = shape((1, width), jnp.float32)
        grad_weight, grad_gain, grad_beta, grad_bias = pl.pallas_call(
            finish_kernel,
            out_shape=(
                shape((own, decoder), jnp.float32),
                vector,
                vector,
                shape((1, decoder), jnp.float32),
            ),
            in_specs=[VMEM] * 2,
            out_specs=(VMEM,) * 4,
            compiler_params=PARAMS,
            cost_estimate=cost(1000000, 300000),
            name="finish",
        )(second, weight_near)
        return (
            grad_rows,
            grad_weight,
            grad_gain.reshape(width),
            grad_beta.reshape(width),
            grad_bias.reshape(decoder),
        )

    return body


def solution(mesh):
    placed = (P(("dp", "bal")), P(("dp", "bal"), None), P(("dp", "bal"), None), P(), P(), P())
    return jax.shard_map(
        make_body(mesh.shape["dp"], mesh.shape["bal"]),
        mesh=mesh,
        in_specs=placed,
        out_specs=(P(("dp", "bal"), None), P(("dp", "bal"), None), P(), P(), P()),
        check_vma=False,
    )
```
